128 devices in a mesh: ctx: 16 (over x, z_lo, core), tp: 8 (over z_hi, y).
Axes of the slice: x: 4, y: 4, z: 4 (z_hi: 2, z_lo: 2; z = z_hi * 2 + z_lo), core: 2. Of those that a mesh axis runs over, the one named last changes fastest.
Arguments:
- query_proj: bfloat16 [4096, 4096], P('ctx', 'tp'), may hold values from -220 to 220
- key_proj: bfloat16 [4096, 4096], P('ctx', 'tp'), may hold values from -6 to 6
- value_proj: bfloat16 [4096, 4096], P('ctx', 'tp'), may hold values from -6 to 6
- out_grad: bfloat16 [4096, 4096], P('ctx', 'tp'), may hold values from -6 to 6
- out_weight: bfloat16 [4096, 4096], P(None, 'tp'), may hold values from -0.125 to 0.125
- block_mask: int32 [32, 32], replicated, may hold values from 0 to 1, as said below
Outputs:
- query_grad: bfloat16 [4096, 4096], P('ctx', 'tp')
- key_grad: bfloat16 [4096, 4096], P('ctx', 'tp')
- value_grad: bfloat16 [4096, 4096], P('ctx', 'tp')
The draws below stay inside these ranges and needn't reach their ends.
Inputs may be any that keep to these rules, and one draw needn't show every extreme that they name: block_mask[i, j] = 1 where blocks i and j belong to the same document or either of them is a global block, else 0; it is symmetric with ones on its diagonal.
All inputs are finite; a program needn't handle non-finite values.
Results may differ from the reference program's by a relative error of at most 0.02.
Values may be sent and summed in bfloat16 or wider, within the bound.
A program may use at most 192 MiB of HBM per device.

```python
import jax
import jax.numpy as jnp
from jax import lax

D = 4096
HEADS = 32
HEAD_DIM = 128
BLOCK = 128
SEQ = 4096
NB = 32


def shared_normal(key):
    return jnp.clip(jax.random.normal(jax.random.fold_in(key, 101), (SEQ, D), jnp.float32), -6.0, 6.0)


def draw_key_proj(key, part):
    shared = shared_normal(key)
    return shared.astype(jnp.bfloat16)


def draw_query_proj(key, part):
    key = jax.random.fold_in(key, 5)
    own = jnp.clip(jax.random.normal(key, (SEQ, D), jnp.float32), -6.0, 6.0)
    return own.astype(jnp.bfloat16)


def draw_block_mask(key, part):
    key = jax.random.fold_in(key, 7)
    first_key, second_key = jax.random.split(key)
    indices = jnp.arange(NB, dtype=jnp.int32)
    starts = jax.random.randint(first_key, (NB,), 0, 4) == 0
    starts = starts | (indices == 0) | (indices == NB // 2)
    documents = jnp.cumsum(starts.astype(jnp.int32))
    globals_flag = (jax.random.randint(second_key, (NB,), 0, 16) == 0) & (indices != 0) & (indices != NB - 1)
    joined = (documents[:, None] == documents[None, :]) | globals_flag[:, None] | globals_flag[None, :]
    return joined.astype(jnp.int32)


def with_spikes(array, own_key, source, target, blocks, factor):
    owner, partner = [(jnp.arange(array.shape[position]) // (array.shape[position] // blocks)).reshape([-1 if axis == position else 1 for axis in range(array.ndim)]) for position in (source, target)]
    chosen = jax.random.permutation(own_key, blocks)[partner]
    strong = (owner == chosen) | (owner == (partner + blocks // 2) % blocks)
    return jnp.where(strong, factor * array, array)


def shard_levels(own_key, dims, cuts, least, largest):
    def one(position, parts):
        steps = jax.random.uniform(jax.random.fold_in(jax.random.fold_in(own_key, 6), position), (parts,), jnp.float32, least / len(cuts), largest / len(cuts))
        return jnp.repeat(jnp.exp(steps), dims[position] // parts).reshape((-1,) + (1,) * (len(dims) - position - 1))

    factor_of = one(*cuts[0])
    for cut in cuts[1:]:
        factor_of = factor_of * one(*cut)
    return factor_of


def noise(key, extent, deviation, reach, cuts=(), kind=jnp.bfloat16):
    result = jax.random.normal(key, extent, jnp.float32) * deviation
    if len(cuts) > 0:
        result = shard_levels(key, extent, cuts, -0.22, 0.18) * result
    return jnp.clip(result, min=-reach, max=reach).astype(kind)


def heavy_noise(key, shape, width, limit, cuts, heavy, kind=jnp.bfloat16):
    values = width * jax.random.normal(key, shape, jnp.float32)
    if cuts:
        values = values * shard_levels(key, shape, cuts, -0.22, 0.18)
    return jnp.clip(with_spikes(values, jax.random.fold_in(key, 3), *heavy), -limit, limit).astype(kind)


def setup_inputs(seed: int = 0) -> dict:
    streams_of = jax.random.split(jax.random.key(seed), 7)
    return {
        "query_proj": draw_query_proj(jax.random.fold_in(streams_of[6], 71), 0),
        "key_proj": draw_key_proj(jax.random.fold_in(streams_of[6], 71), 0),
        "value_proj": noise(streams_of[2], (SEQ, D), 1.0, 6.0, ((0, 16), (1, 8))),
        "out_grad": noise(streams_of[3], (SEQ, D), 1.0, 6.0, ((0, 16), (1, 8))),
        "out_weight": heavy_noise(streams_of[4], (D, D), D ** -0.5, 0.125, ((1, 8),), (1, 0, 8, 2.0)),
        "block_mask": draw_block_mask(jax.random.fold_in(streams_of[6], 71), 0),
    }


def reference(query_proj, key_proj, value_proj, out_grad, out_weight, block_mask):
    attn_grad = lax.dot_general(out_grad, out_weight, (((1,), (1,)), ((), ())), preferred_element_type=jnp.float32).astype(jnp.bfloat16)
    blocks = jnp.arange(SEQ, dtype=jnp.int32) // BLOCK
    allowed = jnp.take(jnp.take(block_mask, blocks, axis=0), blocks, axis=1) == 1
    score_scale = HEAD_DIM ** -0.5

    def by_heads(matrix):
        return matrix.reshape(SEQ, HEADS, HEAD_DIM).transpose(1, 0, 2)

    def to_rows(stacked):
        return stacked.transpose(1, 0, 2).reshape(SEQ, D)

    def one_head(head_data):
        query_head, key_head, value_head, grad_head = head_data
        scores = jnp.dot(query_head, key_head.T, preferred_element_type=jnp.float32) * score_scale
        row_max = jnp.max(jnp.where(allowed, scores, -1e30), axis=1, keepdims=True)
        norm_total = jnp.sum(jnp.where(allowed, jnp.exp(scores - row_max), 0.0), axis=1, keepdims=True)
        log_total = row_max + jnp.log(norm_total)
        probs = jnp.where(allowed, jnp.exp(scores - log_total), 0.0)
        prob_grad = jnp.dot(grad_head, value_head.T, preferred_element_type=jnp.float32)
        row_delta = jnp.sum(probs * prob_grad, axis=1, keepdims=True)
        score_grad = (probs * (prob_grad - row_delta) * score_scale).astype(jnp.bfloat16)
        prob_weights = probs.astype(jnp.bfloat16)
        query_out = jnp.dot(score_grad, key_head, preferred_element_type=jnp.float32).astype(jnp.bfloat16)
        key_out = jnp.dot(score_grad.T, query_head, preferred_element_type=jnp.float32).astype(jnp.bfloat16)
        value_out = jnp.dot(prob_weights.T, grad_head, preferred_element_type=jnp.float32).astype(jnp.bfloat16)
        return query_out, key_out, value_out

    query_out, key_out, value_out = lax.map(one_head, (by_heads(query_proj), by_heads(key_proj), by_heads(value_proj), by_heads(attn_grad)))
    return to_rows(query_out), to_rows(key_out), to_rows(value_out)
```

```python
import functools

import jax
import jax.numpy as jnp
from jax import lax
from jax.experimental import pallas as pl
from jax.experimental.pallas import tpu as pltpu
from jax.sharding import PartitionSpec as P

MESH = pl.DeviceIdType.MESH
HEAD_DIM = 128
BLOCK = 128
ROWS = 256
NX = 4
NEG_FILL = -1e30
SCALE = HEAD_DIM ** (-0.5)
LOG2E = 1.4426950408889634
BF16 = jnp.bfloat16
F32 = jnp.float32
NT = (((1,), (1,)), ((), ()))


def place():
    ctx, tp = lax.axis_index("ctx"), lax.axis_index("tp")
    return (
        lax.div(ctx, 4),
        lax.rem(lax.div(ctx, 2), 2),
        lax.rem(ctx, 2),
        lax.div(tp, 4),
        lax.rem(tp, 4),
    )


def device(x, z, c, zh, y):
    return {"ctx": x * 4 + z * 2 + c, "tp": zh * 4 + y}


def block_rows(x, z, c):
    return pl.ds(pl.multiple_of((x * 4 + z * 2 + c) * ROWS, ROWS), ROWS)


def head_lanes(h):
    return pl.ds(pl.multiple_of(h * HEAD_DIM, HEAD_DIM), HEAD_DIM)


def remote(src, dst, send, recv, to):
    return pltpu.make_async_remote_copy(
        src_ref=src, dst_ref=dst, send_sem=send, recv_sem=recv, device_id=to, device_id_type=MESH
    )


def spread_kernel(
    q_in, k_in, v_in, og_in, w_in,
    q_out, k_out, v_out, g_out,
    og, w, own, relay, relay_got, comb, comb_got, direct, direct_got, z_part, z_got, g_part,
    load_sem, local_sem, y_send, y_recv, z_send, z_recv, g_send, g_recv,
    q_send, q_recv, kv_xsend, kv_xrecv, kv_fsend, kv_frecv,
):
    x, z, c, zh, y = place()
    yp, ym, yo = lax.rem(y + 1, 4), lax.rem(y + 3, 4), lax.rem(y + 2, 4)

    def at_x(d):
        return device(lax.rem(x + d, 4), z, c, zh, y)

    core, zpeer = device(x, z, 1 - c, zh, y), device(x, 1 - z, c, zh, y)
    up, down = device(x, z, c, zh, yp), device(x, z, c, zh, ym)
    zfar = device(x, z, c, 1 - zh, y)

    order = [(yo, 0), (yo, 1), (yp, 0), (ym, 1), (yp, 1), (ym, 0), (y, 0), (y, 1)]
    loads = [pltpu.make_async_copy(og_in, og, load_sem.at[8])]
    for i, (yy, zz) in enumerate(order):
        rows = pl.ds(pl.multiple_of((zz * 4 + yy) * 512, 512), 512)
        loads.append(pltpu.make_async_copy(w_in.at[rows], w.at[i], load_sem.at[i]))
    for load in loads:
        load.start()

    barrier = pltpu.get_barrier_semaphore()
    for peer in (at_x(1), at_x(2), at_x(3), core, zpeer, up, down, zfar):
        pl.semaphore_signal(barrier, inc=1, device_id=peer, device_id_type=MESH)
    pl.semaphore_wait(barrier, 8)

    sent = []

    def go(copy):
        copy.start()
        sent.append(copy)

    def project(i):
        loads[1 + i].wait()
        return lax.dot_general(og[...], w[i], NT, preferred_element_type=F32)

    heads = [lax.rem(x + 1 + i, 4) for i in range(4)]

    def y_copy(kind, zz, i, src, dst, to):
        return remote(
            src.at[zz, heads[i]], dst.at[zz, heads[i]],
            y_send.at[kind, zz, i], y_recv.at[kind, zz, i], to,
        )

    loads[0].wait()
    for zz in range(2):
        part = project(zz)
        for h in range(4):
            relay[zz, h] = part[:, h * 128:(h + 1) * 128].astype(BF16)
    relays = [[y_copy(0, zz, i, relay, relay_got, (up, down)[zz]) for i in range(4)] for zz in range(2)]
    for i in range(4):
        for zz in range(2):
            go(relays[zz][i])

    tensors = [(k_in, k_out), (v_in, v_out)]

    def kv_from_x(t, d):
        src, dst = tensors[t]
        return remote(
            src.at[:, head_lanes(lax.rem(x + d, 4))], dst.at[block_rows(x, z, c)],
            kv_xsend.at[t, d], kv_xrecv.at[t, d], at_x(d),
        )

    def kv_wait_x(t, d):
        dst = tensors[t][1].at[block_rows(lax.rem(x + 4 - d, 4), z, c)]
        remote(dst, dst, kv_xsend.at[t, d], kv_xrecv.at[t, d], core).wait_recv()

    def kv_forward(t, d, route):
        xs = lax.rem(x + 4 - d, 4)
        rows = block_rows(xs, z if route < 2 else 1 - z, c)
        dst = tensors[t][1].at[rows]
        src = tensors[t][0].at[:, head_lanes(x)] if (d == 0 and route < 2) else dst
        return remote(
            src, dst, kv_fsend.at[t, d, route], kv_frecv.at[t, d, route], zpeer if route == 1 else core
        )

    def kv_wait(t, d, route):
        xs = lax.rem(x + 4 - d, 4)
        rows = block_rows(xs, z if route == 0 else 1 - z, c if route == 1 else 1 - c)
        dst = tensors[t][1].at[rows]
        remote(dst, dst, kv_fsend.at[t, d, route], kv_frecv.at[t, d, route], core).wait_recv()

    for t in range(2):
        go(kv_forward(t, 0, 1))
    for d in (1, 3, 2):
        for t in range(2):
            go(kv_from_x(t, d))
    for t in range(2):
        go(kv_forward(t, 0, 0))
    local = []
    for t in range(2):
        local.append(pltpu.make_async_copy(
            tensors[t][0].at[:, head_lanes(x)], tensors[t][1].at[block_rows(x, z, c)], local_sem.at[t]))
    q_rows = pl.ds(pl.multiple_of(x * ROWS, ROWS), ROWS)
    local.append(pltpu.make_async_copy(q_in.at[:, head_lanes(x)], q_out.at[q_rows], local_sem.at[2]))
    for copy in local:
        copy.start()
    q_copies = [
        remote(q_in.at[:, head_lanes(lax.rem(x + d, 4))], q_out.at[q_rows], q_send.at[d], q_recv.at[d], at_x(d))
        for d in (1, 2, 3)
    ]

    for i in range(2, 8):
        zz = order[i][1]
        part = project(i)
        for h in range(4):
            piece = part[:, h * 128:(h + 1) * 128]
            if i in (4, 5):
                direct[zz, h] = piece.astype(BF16)
            else:
                own[0 if i < 4 else 1, zz, h] = piece

    def combine(i):
        h = heads[i]
        for zz in range(2):
            relays[zz][i].wait_recv()
            comb[zz, h] = (relay_got[zz, h].astype(F32) + own[0, zz, h]).astype(BF16)
            go(y_copy(1, zz, i, comb, comb_got, (up, down)[zz]))
        for zz in range(2):
            go(y_copy(2, zz, i, direct, direct_got, (down, up)[zz]))

    z_copies = [
        remote(z_part.at[heads[i]], z_got.at[heads[i]], z_send.at[i], z_recv.at[i], zfar) for i in range(4)
    ]

    def finish_y(i):
        h = heads[i]
        for zz in range(2):
            y_copy(1, zz, i, comb, comb_got, up).wait_recv()
            y_copy(2, zz, i, direct, direct_got, up).wait_recv()
        far = own[1, 1 - zh, h] + comb_got[1 - zh, h].astype(F32) + direct_got[1 - zh, h].astype(F32)
        z_part[h] = far.astype(BF16)
        go(z_copies[i])
        own[1, zh, h] = own[1, zh, h] + comb_got[zh, h].astype(F32) + direct_got[zh, h].astype(F32)

    def finish_z(i):
        h = heads[i]
        z_copies[i].wait_recv()
        g_part[h] = (own[1, zh, h] + z_got[h].astype(F32)).astype(BF16)
        if i < 3:
            go(remote(g_part.at[h], g_out.at[q_rows], g_send.at[i], g_recv.at[i], at_x(i + 1)))
        else:
            copy = pltpu.make_async_copy(g_part.at[h], g_out.at[q_rows], local_sem.at[3])
            copy.start()
            local.append(copy)

    def pass_on(d):
        for t in range(2):
            kv_wait_x(t, d)
            go(kv_forward(t, d, 1))
            go(kv_forward(t, d, 0))

    def pass_z(d):
        for t in range(2):
            kv_wait(t, d, 1)
            go(kv_forward(t, d, 2))

    combine(0)
    pass_on(1)
    combine(1)
    pass_on(3)
    for copy in q_copies:
        go(copy)
    combine(2)
    pass_z(0)
    combine(3)
    pass_on(2)
    pass_z(1)
    finish_y(0)
    pass_z(3)
    finish_y(1)
    finish_z(0)
    finish_y(2)
    finish_z(1)
    pass_z(2)
    finish_y(3)
    finish_z(2)
    finish_z(3)

    for d in range(4):
        for t in range(2):
            kv_wait(t, d, 0)
            kv_wait(t, d, 2)
    for copy in q_copies:
        copy.wait_recv()
    for i in range(3):
        rows = pl.ds(pl.multiple_of(lax.rem(x + 3 - i, 4) * ROWS, ROWS), ROWS)
        dst = g_out.at[rows]
        remote(dst, dst, g_send.at[i], g_recv.at[i], core).wait_recv()
    for copy in local:
        copy.wait()
    for copy in sent:
        copy.wait_send()


def spread(q, k, v, og, w):
    dma = pltpu.SemaphoreType.DMA
    hbm = pl.BlockSpec(memory_space=pltpu.HBM)
    return pl.pallas_call(
        spread_kernel,
        out_shape=(
            jax.ShapeDtypeStruct((NX * ROWS, 128), BF16),
            jax.ShapeDtypeStruct((16 * ROWS, 128), BF16),
            jax.ShapeDtypeStruct((16 * ROWS, 128), BF16),
            jax.ShapeDtypeStruct((NX * ROWS, 128), BF16),
        ),
        in_specs=[hbm] * 5,
        out_specs=(hbm,) * 4,
        scratch_shapes=[
            pltpu.VMEM((ROWS, 512), BF16),
            pltpu.VMEM((8, 512, 512), BF16),
            pltpu.VMEM((2, 2, 4, ROWS, 128), F32),
            *[pltpu.VMEM((2, 4, ROWS, 128), BF16)] * 6,
            *[pltpu.VMEM((4, ROWS, 128), BF16)] * 3,
            dma((9,)), dma((4,)),
            dma((3, 2, 4)), dma((3, 2, 4)),
            dma((4,)), dma((4,)), dma((3,)), dma((3,)),
            dma((4,)), dma((4,)),
            dma((2, 4)), dma((2, 4)), dma((2, 4, 3)), dma((2, 4, 3)),
        ],
        compiler_params=pltpu.CompilerParams(
            collective_id=0, has_side_effects=True, vmem_limit_bytes=48 << 20
        ),
        name="spread",
    )(q, k, v, og, w)


GROUP = 4


def attention_kernel(mask, q, g, k, v, dq, dk, dv, s_scr, p_scr, dk_acc, dv_acc, picks, bias):
    ctx = lax.axis_index("ctx")
    zc = lax.rem(ctx, 4)
    dk_acc[...] = jnp.zeros_like(dk_acc)
    dv_acc[...] = jnp.zeros_like(dv_acc)

    def tile(i, carry):
        first = (i * 4 + zc) * 2
        def pick(b, count):
            m0, m1 = mask[first, b] == 1, mask[first + 1, b] == 1
            picks[count] = b
            bias[0, count] = jnp.where(m0, 0.0, NEG_FILL)
            bias[1, count] = jnp.where(m1, 0.0, NEG_FILL)
            return count + jnp.where(m0 | m1, 1, 0)

        count = lax.fori_loop(0, 32, pick, 0)
        steps = lax.div(count + GROUP - 1, GROUP)

        def pad(b, carry):
            picks[b] = 0
            bias[0, b] = NEG_FILL
            bias[1, b] = NEG_FILL
            return carry

        lax.fori_loop(count, steps * GROUP, pad, 0)

        q_rows = pl.ds(pl.multiple_of(i * ROWS, ROWS), ROWS)
        q_tile, g_tile = q[q_rows, :], g[q_rows, :]

        def rows_of(j, n):
            return pl.ds(pl.multiple_of(picks[j * GROUP + n] * BLOCK, BLOCK), BLOCK)

        def scores(j, top):
            k_cat = jnp.concatenate([k[rows_of(j, n), :] for n in range(GROUP)], axis=0)
            v_cat = jnp.concatenate([v[rows_of(j, n), :] for n in range(GROUP)], axis=0)
            s = lax.dot_general(k_cat, q_tile, NT, preferred_element_type=F32)
            p_scr[j] = lax.dot_general(v_cat, g_tile, NT, preferred_element_type=F32)
            for n in range(GROUP):
                fill = jnp.concatenate(
                    [jnp.full((1, 128), bias[a, j * GROUP + n], F32) for a in range(2)], axis=1
                )
                part = s[n * BLOCK:(n + 1) * BLOCK] * (SCALE * LOG2E) + fill
                s_scr[j, n * BLOCK:(n + 1) * BLOCK, :] = part
                top = jnp.maximum(top, jnp.max(part.reshape(BLOCK // 8, 8, ROWS), axis=0))
            return top

        top = lax.fori_loop(0, steps, scores, jnp.full((8, ROWS), NEG_FILL, F32))
        top = jnp.max(top, axis=0, keepdims=True)

        def sums(j, carry):
            total, weighted = carry
            e = jnp.exp2(s_scr[j] - top)
            s_scr[j] = e
            total = total + jnp.sum(e.reshape(GROUP * BLOCK // 8, 8, ROWS), axis=0)
            weighted = weighted + jnp.sum((e * p_scr[j]).reshape(GROUP * BLOCK // 8, 8, ROWS), axis=0)
            return total, weighted

        zero = jnp.zeros((8, ROWS), F32)
        total, weighted = lax.fori_loop(0, steps, sums, (zero, zero))
        inverse = 1.0 / jnp.sum(total, axis=0, keepdims=True)
        delta = jnp.sum(weighted, axis=0, keepdims=True) * inverse

        def grads(j, dq_acc):
            p = s_scr[j] * inverse
            ds = (p * (p_scr[j] - delta)).astype(BF16)
            p = p.astype(BF16)
            k_cat = jnp.concatenate([k[rows_of(j, n), :] for n in range(GROUP)], axis=0)
            dv_part = jnp.dot(p, g_tile, preferred_element_type=F32)
            dk_part = jnp.dot(ds, q_tile, preferred_element_type=F32)
            dq_acc = dq_acc + lax.dot_general(
                ds, k_cat, (((0,), (0,)), ((), ())), preferred_element_type=F32
            )
            for n in range(GROUP):
                rows = rows_of(j, n)
                dk_acc[rows, :] += dk_part[n * BLOCK:(n + 1) * BLOCK]
                dv_acc[rows, :] += dv_part[n * BLOCK:(n + 1) * BLOCK]
            return dq_acc

        dq_acc = lax.fori_loop(0, steps, grads, jnp.zeros((ROWS, 128), F32))
        dq[q_rows, :] = (dq_acc * SCALE).astype(BF16)
        return carry

    lax.fori_loop(0, NX, tile, 0)
    dk[...] = (dk_acc[...] * SCALE).astype(BF16)
    dv[...] = dv_acc[...].astype(BF16)


def attention(mask, q, g, k, v):
    vmem = pl.BlockSpec(memory_space=pltpu.VMEM)
    return pl.pallas_call(
        attention_kernel,
        out_shape=(
            jax.ShapeDtypeStruct((NX * ROWS, 128), BF16),
            jax.ShapeDtypeStruct((16 * ROWS, 128), BF16),
            jax.ShapeDtypeStruct((16 * ROWS, 128), BF16),
        ),
        in_specs=[pl.BlockSpec(memory_space=pltpu.SMEM)] + [vmem] * 4,
        out_specs=(vmem,) * 3,
        scratch_shapes=[
            pltpu.VMEM((32 // GROUP, GROUP * BLOCK, ROWS), F32),
            pltpu.VMEM((32 // GROUP, GROUP * BLOCK, ROWS), F32),
            pltpu.VMEM((16 * ROWS, 128), F32),
            pltpu.VMEM((16 * ROWS, 128), F32),
            pltpu.SMEM((64,), jnp.int32),
            pltpu.SMEM((2, 64), F32),
        ],
        compiler_params=pltpu.CompilerParams(vmem_limit_bytes=48 << 20),
        name="attention",
    )(mask, q, g, k, v)


def collect_kernel(
    dq_in, dk_in, dv_in,
    dq_out, dk_out, dv_out,
    own, core_got, z_part, z_got, part,
    load_sem, local_sem, core_send, core_recv, z_send, z_recv, x_send, x_recv, q_send, q_recv,
):
    x, z, c, zh, y = place()

    def at_x(d):
        return device(lax.rem(x + d, 4), z, c, zh, y)

    core, zpeer = device(x, z, 1 - c, zh, y), device(x, 1 - z, c, zh, y)
    tensors = [(dk_in, dk_out), (dv_in, dv_out)]
    order = (1, 3, 2, 0)

    loads = {}
    for far in (1, 0):
        for d in order:
            for t in range(2):
                rows = block_rows(lax.rem(x + d, 4), 1 - z if far else z, c)
                loads[far, d, t] = pltpu.make_async_copy(
                    tensors[t][0].at[rows], own.at[far, d, t], load_sem.at[far, d, t])
                loads[far, d, t].start()

    barrier = pltpu.get_barrier_semaphore()
    for peer in (at_x(1), at_x(2), at_x(3), core, zpeer):
        pl.semaphore_signal(barrier, inc=1, device_id=peer, device_id_type=MESH)
    pl.semaphore_wait(barrier, 5)

    sent = []

    def go(copy):
        copy.start()
        sent.append(copy)

    to_core = {}
    for far in (1, 0):
        for d in order:
            for t in range(2):
                rows = block_rows(lax.rem(x + d, 4), 1 - z if far else z, 1 - c)
                to_core[far, d, t] = remote(
                    tensors[t][0].at[rows], core_got.at[far, d, t],
                    core_send.at[far, d, t], core_recv.at[far, d, t], core)
                go(to_core[far, d, t])

    q_copies = [
        remote(
            dq_in.at[pl.ds(pl.multiple_of(lax.rem(x + d, 4) * ROWS, ROWS), ROWS)],
            dq_out.at[:, head_lanes(x)], q_send.at[d], q_recv.at[d], at_x(d))
        for d in (1, 2, 3)
    ]
    for copy in q_copies:
        go(copy)
    local = [pltpu.make_async_copy(
        dq_in.at[pl.ds(pl.multiple_of(x * ROWS, ROWS), ROWS)], dq_out.at[:, head_lanes(x)], local_sem.at[2])]
    local[0].start()

    to_z = {}
    for d in order:
        for t in range(2):
            loads[1, d, t].wait()
            to_core[1, d, t].wait_recv()
            z_part[d, t] = (own[1, d, t].astype(F32) + core_got[1, d, t].astype(F32)).astype(BF16)
            to_z[d, t] = remote(z_part.at[d, t], z_got.at[d, t], z_send.at[d, t], z_recv.at[d, t], zpeer)
            go(to_z[d, t])
    for d in order:
        for t in range(2):
            loads[0, d, t].wait()
            to_core[0, d, t].wait_recv()
            to_z[d, t].wait_recv()
            part[d, t] = (
                own[0, d, t].astype(F32) + core_got[0, d, t].astype(F32) + z_got[d, t].astype(F32)
            ).astype(BF16)
            dst = tensors[t][1].at[:, head_lanes(x)]
            if d == 0:
                copy = pltpu.make_async_copy(part.at[d, t], dst, local_sem.at[t])
                copy.start()
                local.append(copy)
            else:
                go(remote(part.at[d, t], dst, x_send.at[d, t], x_recv.at[d, t], at_x(d)))

    for d in (1, 2, 3):
        lanes = head_lanes(lax.rem(x + 4 - d, 4))
        for t in range(2):
            dst = tensors[t][1].at[:, lanes]
            remote(dst, dst, x_send.at[d, t], x_recv.at[d, t], core).wait_recv()
        dst = dq_out.at[:, lanes]
        remote(dst, dst, q_send.at[d], q_recv.at[d], core).wait_recv()
    for copy in local:
        copy.wait()
    for copy in sent:
        copy.wait_send()


def collect(dq, dk, dv):
    dma = pltpu.SemaphoreType.DMA
    hbm = pl.BlockSpec(memory_space=pltpu.HBM)
    piece = (ROWS, 128)
    return pl.pallas_call(
        collect_kernel,
        out_shape=(jax.ShapeDtypeStruct((ROWS, 512), BF16),) * 3,
        in_specs=[hbm] * 3,
        out_specs=(hbm,) * 3,
        scratch_shapes=[
            pltpu.VMEM((2, 4, 2, *piece), BF16),
            pltpu.VMEM((2, 4, 2, *piece), BF16),
            pltpu.VMEM((4, 2, *piece), BF16),
            pltpu.VMEM((4, 2, *piece), BF16),
            pltpu.VMEM((4, 2, *piece), BF16),
            dma((2, 4, 2)), dma((3,)),
            dma((2, 4, 2)), dma((2, 4, 2)),
            dma((4, 2)), dma((4, 2)),
            dma((4, 2)), dma((4, 2)),
            dma((4,)), dma((4,)),
        ],
        compiler_params=pltpu.CompilerParams(
            collective_id=1, has_side_effects=True, vmem_limit_bytes=48 << 20
        ),
        name="collect",
    )(dq, dk, dv)


def per_device(query_proj, key_proj, value_proj, out_grad, out_weight, block_mask):
    q, k, v, g = spread(query_proj, key_proj, value_proj, out_grad, out_weight)
    dq, dk, dv = attention(block_mask, q, g, k, v)
    return collect(dq, dk, dv)


def solution(mesh):
    placed = (P("ctx", "tp"), P("ctx", "tp"), P("ctx", "tp"), P("ctx", "tp"), P(None, "tp"), P())
    return jax.shard_map(
        per_device,
        mesh=mesh,
        in_specs=placed,
        out_specs=(P("ctx", "tp"), P("ctx", "tp"), P("ctx", "tp")),
        check_vma=False,
    )
```

```python
import functools

import jax
import jax.numpy as jnp
from jax import lax
from jax.experimental import pallas as pl
from jax.experimental.pallas import tpu as pltpu
from jax.sharding import PartitionSpec as P

MESH = pl.DeviceIdType.MESH
HEAD_DIM = 128
BLOCK = 128
ROWS = 256
NX = 4
NEG_FILL = -1e30
SCALE = HEAD_DIM ** (-0.5)
LOG2E = 1.4426950408889634
BF16 = jnp.bfloat16
F32 = jnp.float32
NT = (((1,), (1,)), ((), ()))


def place():
    ctx, tp = lax.axis_index("ctx"), lax.axis_index("tp")
    return (
        lax.div(ctx, 4),
        lax.rem(lax.div(ctx, 2), 2),
        lax.rem(ctx, 2),
        lax.div(tp, 4),
        lax.rem(tp, 4),
    )


def device(x, z, c, zh, y):
    return {"ctx": x * 4 + z * 2 + c, "tp": zh * 4 + y}


def block_rows(x, z, c):
    return pl.ds(pl.multiple_of((x * 4 + z * 2 + c) * ROWS, ROWS), ROWS)


def head_lanes(h):
    return pl.ds(pl.multiple_of(h * HEAD_DIM, HEAD_DIM), HEAD_DIM)


def remote(src, dst, send, recv, to):
    return pltpu.make_async_remote_copy(
        src_ref=src, dst_ref=dst, send_sem=send, recv_sem=recv, device_id=to, device_id_type=MESH
    )


def spread_kernel(
    q_in, k_in, v_in, og_in, w_in,
    q_out, k_out, v_out, g_out,
    og, w, own, relay, relay_got, comb, comb_got, direct, direct_got, z_part, z_got, g_part,
    load_sem, local_sem, y_send, y_recv, z_send, z_recv, g_send, g_recv,
    q_send, q_recv, kv_xsend, kv_xrecv, kv_fsend, kv_frecv,
):
    x, z, c, zh, y = place()
    yp, ym, yo = lax.rem(y + 1, 4), lax.rem(y + 3, 4), lax.rem(y + 2, 4)

    def at_x(d):
        return device(lax.rem(x + d, 4), z, c, zh, y)

    core, zpeer = device(x, z, 1 - c, zh, y), device(x, 1 - z, c, zh, y)
    up, down = device(x, z, c, zh, yp), device(x, z, c, zh, ym)
    zfar = device(x, z, c, 1 - zh, y)

    order = [(yo, 0), (yo, 1), (yp, 0), (ym, 1), (yp, 1), (ym, 0), (y, 0), (y, 1)]
    loads = [pltpu.make_async_copy(og_in, og, load_sem.at[8])]
    for i, (yy, zz) in enumerate(order):
        rows = pl.ds(pl.multiple_of((zz * 4 + yy) * 512, 512), 512)
        loads.append(pltpu.make_async_copy(w_in.at[rows], w.at[i], load_sem.at[i]))
    for load in loads:
        load.start()

    barrier = pltpu.get_barrier_semaphore()
    for peer in (at_x(1), at_x(2), at_x(3), core, zpeer, up, down, zfar):
        pl.semaphore_signal(barrier, inc=1, device_id=peer, device_id_type=MESH)
    pl.semaphore_wait(barrier, 8)

    sent = []

    def go(copy):
        copy.start()
        sent.append(copy)

    def project(i):
        loads[1 + i].wait()
        return lax.dot_general(og[...], w[i], NT, preferred_element_type=F32)

    heads = [lax.rem(x + 1 + i, 4) for i in range(4)]

    def y_copy(kind, zz, i, src, dst, to):
        return remote(
            src.at[zz, heads[i]], dst.at[zz, heads[i]],
            y_send.at[kind, zz, i], y_recv.at[kind, zz, i], to,
        )

    loads[0].wait()
    for zz in range(2):
        part = project(zz)
        for h in range(4):
            relay[zz, h] = part[:, h * 128:(h + 1) * 128].astype(BF16)
    relays = [[y_copy(0, zz, i, relay, relay_got, (up, down)[zz]) for i in range(4)] for zz in range(2)]
    for i in range(4):
        for zz in range(2):
            go(relays[zz][i])

    tensors = [(k_in, k_out), (v_in, v_out)]

    def kv_from_x(t, d):
        src, dst = tensors[t]
        return remote(
            src.at[:, head_lanes(lax.rem(x + d, 4))], dst.at[block_rows(x, z, c)],
            kv_xsend.at[t, d], kv_xrecv.at[t, d], at_x(d),
        )

    def kv_wait_x(t, d):
        dst = tensors[t][1].at[block_rows(lax.rem(x + 4 - d, 4), z, c)]
        remote(dst, dst, kv_xsend.at[t, d], kv_xrecv.at[t, d], core).wait_recv()

    def kv_forward(t, d, route):
        xs = lax.rem(x + 4 - d, 4)
        rows = block_rows(xs, z if route < 2 else 1 - z, c)
        dst = tensors[t][1].at[rows]
        src = tensors[t][0].at[:, head_lanes(x)] if (d == 0 and route < 2) else dst
        return remote(
            src, dst, kv_fsend.at[t, d, route], kv_frecv.at[t, d, route], zpeer if route == 1 else core
        )

    def kv_wait(t, d, route):
        xs = lax.rem(x + 4 - d, 4)
        rows = block_rows(xs, z if route == 0 else 1 - z, c if route == 1 else 1 - c)
        dst = tensors[t][1].at[rows]
        remote(dst, dst, kv_fsend.at[t, d, route], kv_frecv.at[t, d, route], core).wait_recv()

    for t in range(2):
        go(kv_forward(t, 0, 1))
    for d in (1, 3, 2):
        for t in range(2):
            go(kv_from_x(t, d))
    for t in range(2):
        go(kv_forward(t, 0, 0))
    local = []
    for t in range(2):
        local.append(pltpu.make_async_copy(
            tensors[t][0].at[:, head_lanes(x)], tensors[t][1].at[block_rows(x, z, c)], local_sem.at[t]))
    q_rows = pl.ds(pl.multiple_of(x * ROWS, ROWS), ROWS)
    local.append(pltpu.make_async_copy(q_in.at[:, head_lanes(x)], q_out.at[q_rows], local_sem.at[2]))
    for copy in local:
        copy.start()
    q_copies = [
        remote(q_in.at[:, head_lanes(lax.rem(x + d, 4))], q_out.at[q_rows], q_send.at[d], q_recv.at[d], at_x(d))
        for d in (1, 2, 3)
    ]

    for i in range(2, 8):
        zz = order[i][1]
        part = project(i)
        for h in range(4):
            piece = part[:, h * 128:(h + 1) * 128]
            if i in (4, 5):
                direct[zz, h] = piece.astype(BF16)
            else:
                own[0 if i < 4 else 1, zz, h] = piece

    def combine(i):
        h = heads[i]
        for zz in range(2):
            relays[zz][i].wait_recv()
            comb[zz, h] = (relay_got[zz, h].astype(F32) + own[0, zz, h]).astype(BF16)
            go(y_copy(1, zz, i, comb, comb_got, (up, down)[zz]))
        for zz in range(2):
            go(y_copy(2, zz, i, direct, direct_got, (down, up)[zz]))

    z_copies = [
        remote(z_part.at[heads[i]], z_got.at[heads[i]], z_send.at[i], z_recv.at[i], zfar) for i in range(4)
    ]

    def finish_y(i):
        h = heads[i]
        for zz in range(2):
            y_copy(1, zz, i, comb, comb_got, up).wait_recv()
            y_copy(2, zz, i, direct, direct_got, up).wait_recv()
        far = own[1, 1 - zh, h] + comb_got[1 - zh, h].astype(F32) + direct_got[1 - zh, h].astype(F32)
        z_part[h] = far.astype(BF16)
        go(z_copies[i])
        own[1, zh, h] = own[1, zh, h] + comb_got[zh, h].astype(F32) + direct_got[zh, h].astype(F32)

    def finish_z(i):
        h = heads[i]
        z_copies[i].wait_recv()
        g_part[h] = (own[1, zh, h] + z_got[h].astype(F32)).astype(BF16)
        if i < 3:
            go(remote(g_part.at[h], g_out.at[q_rows], g_send.at[i], g_recv.at[i], at_x(i + 1)))
        else:
            copy = pltpu.make_async_copy(g_part.at[h], g_out.at[q_rows], local_sem.at[3])
            copy.start()
            local.append(copy)

    def pass_on(d):
        for t in range(2):
            kv_wait_x(t, d)
            go(kv_forward(t, d, 1))
            go(kv_forward(t, d, 0))

    def pass_z(d):
        for t in range(2):
            kv_wait(t, d, 1)
            go(kv_forward(t, d, 2))

    combine(0)
    pass_on(1)
    combine(1)
    pass_on(3)
    for copy in q_copies:
        go(copy)
    combine(2)
    pass_z(0)
    combine(3)
    pass_on(2)
    pass_z(1)
    finish_y(0)
    pass_z(3)
    finish_y(1)
    finish_z(0)
    finish_y(2)
    finish_z(1)
    pass_z(2)
    finish_y(3)
    finish_z(2)
    finish_z(3)

    for d in range(4):
        for t in range(2):
            kv_wait(t, d, 0)
            kv_wait(t, d, 2)
    for copy in q_copies:
        copy.wait_recv()
    for i in range(3):
        rows = pl.ds(pl.multiple_of(lax.rem(x + 3 - i, 4) * ROWS, ROWS), ROWS)
        dst = g_out.at[rows]
        remote(dst, dst, g_send.at[i], g_recv.at[i], core).wait_recv()
    for copy in local:
        copy.wait()
    for copy in sent:
        copy.wait_send()


def spread(q, k, v, og, w):
    dma = pltpu.SemaphoreType.DMA
    hbm = pl.BlockSpec(memory_space=pltpu.HBM)
    return pl.pallas_call(
        spread_kernel,
        out_shape=(
            jax.ShapeDtypeStruct((NX * ROWS, 128), BF16),
            jax.ShapeDtypeStruct((16 * ROWS, 128), BF16),
            jax.ShapeDtypeStruct((16 * ROWS, 128), BF16),
            jax.ShapeDtypeStruct((NX * ROWS, 128), BF16),
        ),
        in_specs=[hbm] * 5,
        out_specs=(hbm,) * 4,
        scratch_shapes=[
            pltpu.VMEM((ROWS, 512), BF16),
            pltpu.VMEM((8, 512, 512), BF16),
            pltpu.VMEM((2, 2, 4, ROWS, 128), F32),
            *[pltpu.VMEM((2, 4, ROWS, 128), BF16)] * 6,
            *[pltpu.VMEM((4, ROWS, 128), BF16)] * 3,
            dma((9,)), dma((4,)),
            dma((3, 2, 4)), dma((3, 2, 4)),
            dma((4,)), dma((4,)), dma((3,)), dma((3,)),
            dma((4,)), dma((4,)),
            dma((2, 4)), dma((2, 4)), dma((2, 4, 3)), dma((2, 4, 3)),
        ],
        compiler_params=pltpu.CompilerParams(
            collective_id=0, has_side_effects=True, vmem_limit_bytes=48 << 20
        ),
        name="spread",
    )(q, k, v, og, w)


GROUP = 4


def attention_kernel(mask, q, g, k, v, dq, dk, dv, s_scr, p_scr, dk_acc, dv_acc, picks, bias):
    ctx = lax.axis_index("ctx")
    zc = lax.rem(ctx, 4)
    dk_acc[...] = jnp.zeros_like(dk_acc)
    dv_acc[...] = jnp.zeros_like(dv_acc)

    def tile(i, carry):
        first = (i * 4 + zc) * 2
        def pick(b, count):
            m0, m1 = mask[first, b] == 1, mask[first + 1, b] == 1
            picks[count] = b
            bias[0, count] = jnp.where(m0, 0.0, NEG_FILL)
            bias[1, count] = jnp.where(m1, 0.0, NEG_FILL)
            return count + jnp.where(m0 | m1, 1, 0)

        count = lax.fori_loop(0, 32, pick, 0, unroll=8)
        steps = lax.div(count + GROUP - 1, GROUP)

        def pad(b, carry):
            picks[b] = 0
            bias[0, b] = NEG_FILL
            bias[1, b] = NEG_FILL
            return carry

        lax.fori_loop(count, steps * GROUP, pad, 0)

        q_rows = pl.ds(pl.multiple_of(i * ROWS, ROWS), ROWS)
        q_tile, g_tile = q[q_rows, :], g[q_rows, :]

        def rows_of(j, n):
            return pl.ds(pl.multiple_of(picks[j * GROUP + n] * BLOCK, BLOCK), BLOCK)

        def scores(j, top):
            k_cat = jnp.concatenate([k[rows_of(j, n), :] for n in range(GROUP)], axis=0)
            v_cat = jnp.concatenate([v[rows_of(j, n), :] for n in range(GROUP)], axis=0)
            s = lax.dot_general(k_cat, q_tile, NT, preferred_element_type=F32)
            p_scr[j] = lax.dot_general(v_cat, g_tile, NT, preferred_element_type=F32)
            for n in range(GROUP):
                fill = jnp.concatenate(
                    [jnp.full((1, 128), bias[a, j * GROUP + n], F32) for a in range(2)], axis=1
                )
                part = s[n * BLOCK:(n + 1) * BLOCK] * (SCALE * LOG2E) + fill
                s_scr[j, n * BLOCK:(n + 1) * BLOCK, :] = part
                top = jnp.maximum(top, jnp.max(part.reshape(BLOCK // 8, 8, ROWS), axis=0))
            return top

        top = lax.fori_loop(0, steps, scores, jnp.full((8, ROWS), NEG_FILL, F32))
        top = jnp.max(top, axis=0, keepdims=True)

        def sums(j, carry):
            total, weighted = carry
            e = jnp.exp2(s_scr[j] - top)
            s_scr[j] = e
            total = total + jnp.sum(e.reshape(GROUP * BLOCK // 8, 8, ROWS), axis=0)
            weighted = weighted + jnp.sum((e * p_scr[j]).reshape(GROUP * BLOCK // 8, 8, ROWS), axis=0)
            return total, weighted

        zero = jnp.zeros((8, ROWS), F32)
        total, weighted = lax.fori_loop(0, steps, sums, (zero, zero))
        inverse = 1.0 / jnp.sum(total, axis=0, keepdims=True)
        delta = jnp.sum(weighted, axis=0, keepdims=True) * inverse

        def grads(j, dq_acc):
            p = s_scr[j] * inverse
            ds = (p * (p_scr[j] - delta)).astype(BF16)
            p = p.astype(BF16)
            k_cat = jnp.concatenate([k[rows_of(j, n), :] for n in range(GROUP)], axis=0)
            dv_part = jnp.dot(p, g_tile, preferred_element_type=F32)
            dk_part = jnp.dot(ds, q_tile, preferred_element_type=F32)
            dq_acc = dq_acc + lax.dot_general(
                ds, k_cat, (((0,), (0,)), ((), ())), preferred_element_type=F32
            )
            for n in range(GROUP):
                rows = rows_of(j, n)
                dk_acc[rows, :] += dk_part[n * BLOCK:(n + 1) * BLOCK]
                dv_acc[rows, :] += dv_part[n * BLOCK:(n + 1) * BLOCK]
            return dq_acc

        dq_acc = lax.fori_loop(0, steps, grads, jnp.zeros((ROWS, 128), F32))
        dq[q_rows, :] = (dq_acc * SCALE).astype(BF16)
        return carry

    lax.fori_loop(0, NX, tile, 0)
    dk[...] = (dk_acc[...] * SCALE).astype(BF16)
    dv[...] = dv_acc[...].astype(BF16)


def attention(mask, q, g, k, v):
    vmem = pl.BlockSpec(memory_space=pltpu.VMEM)
    return pl.pallas_call(
        attention_kernel,
        out_shape=(
            jax.ShapeDtypeStruct((NX * ROWS, 128), BF16),
            jax.ShapeDtypeStruct((16 * ROWS, 128), BF16),
            jax.ShapeDtypeStruct((16 * ROWS, 128), BF16),
        ),
        in_specs=[pl.BlockSpec(memory_space=pltpu.SMEM)] + [vmem] * 4,
        out_specs=(vmem,) * 3,
        scratch_shapes=[
            pltpu.VMEM((32 // GROUP, GROUP * BLOCK, ROWS), F32),
            pltpu.VMEM((32 // GROUP, GROUP * BLOCK, ROWS), F32),
            pltpu.VMEM((16 * ROWS, 128), F32),
            pltpu.VMEM((16 * ROWS, 128), F32),
            pltpu.SMEM((64,), jnp.int32),
            pltpu.SMEM((2, 64), F32),
        ],
        compiler_params=pltpu.CompilerParams(vmem_limit_bytes=48 << 20),
        name="attention",
    )(mask, q, g, k, v)


def collect_kernel(
    dq_in, dk_in, dv_in,
    dq_out, dk_out, dv_out,
    own, core_got, z_part, z_got, part,
    load_sem, local_sem, core_send, core_recv, z_send, z_recv, x_send, x_recv, q_send, q_recv,
):
    x, z, c, zh, y = place()

    def at_x(d):
        return device(lax.rem(x + d, 4), z, c, zh, y)

    core, zpeer = device(x, z, 1 - c, zh, y), device(x, 1 - z, c, zh, y)
    tensors = [(dk_in, dk_out), (dv_in, dv_out)]
    order = (1, 3, 2, 0)

    loads = {}
    for far in (1, 0):
        for d in order:
            for t in range(2):
                rows = block_rows(lax.rem(x + d, 4), 1 - z if far else z, c)
                loads[far, d, t] = pltpu.make_async_copy(
                    tensors[t][0].at[rows], own.at[far, d, t], load_sem.at[far, d, t])
                loads[far, d, t].start()

    barrier = pltpu.get_barrier_semaphore()
    for peer in (at_x(1), at_x(2), at_x(3), core, zpeer):
        pl.semaphore_signal(barrier, inc=1, device_id=peer, device_id_type=MESH)
    pl.semaphore_wait(barrier, 5)

    sent = []

    def go(copy):
        copy.start()
        sent.append(copy)

    to_core = {}
    for far in (1, 0):
        for d in order:
            for t in range(2):
                rows = block_rows(lax.rem(x + d, 4), 1 - z if far else z, 1 - c)
                to_core[far, d, t] = remote(
                    tensors[t][0].at[rows], core_got.at[far, d, t],
                    core_send.at[far, d, t], core_recv.at[far, d, t], core)
                go(to_core[far, d, t])

    q_copies = [
        remote(
            dq_in.at[pl.ds(pl.multiple_of(lax.rem(x + d, 4) * ROWS, ROWS), ROWS)],
            dq_out.at[:, head_lanes(x)], q_send.at[d], q_recv.at[d], at_x(d))
        for d in (1, 2, 3)
    ]
    for copy in q_copies:
        go(copy)
    local = [pltpu.make_async_copy(
        dq_in.at[pl.ds(pl.multiple_of(x * ROWS, ROWS), ROWS)], dq_out.at[:, head_lanes(x)], local_sem.at[2])]
    local[0].start()

    to_z = {}
    for d in order:
        for t in range(2):
            loads[1, d, t].wait()
            to_core[1, d, t].wait_recv()
            z_part[d, t] = (own[1, d, t].astype(F32) + core_got[1, d, t].astype(F32)).astype(BF16)
            to_z[d, t] = remote(z_part.at[d, t], z_got.at[d, t], z_send.at[d, t], z_recv.at[d, t], zpeer)
            go(to_z[d, t])
    for d in order:
        for t in range(2):
            loads[0, d, t].wait()
            to_core[0, d, t].wait_recv()
            to_z[d, t].wait_recv()
            part[d, t] = (
                own[0, d, t].astype(F32) + core_got[0, d, t].astype(F32) + z_got[d, t].astype(F32)
            ).astype(BF16)
            dst = tensors[t][1].at[:, head_lanes(x)]
            if d == 0:
                copy = pltpu.make_async_copy(part.at[d, t], dst, local_sem.at[t])
                copy.start()
                local.append(copy)
            else:
                go(remote(part.at[d, t], dst, x_send.at[d, t], x_recv.at[d, t], at_x(d)))

    for d in (1, 2, 3):
        lanes = head_lanes(lax.rem(x + 4 - d, 4))
        for t in range(2):
            dst = tensors[t][1].at[:, lanes]
            remote(dst, dst, x_send.at[d, t], x_recv.at[d, t], core).wait_recv()
        dst = dq_out.at[:, lanes]
        remote(dst, dst, q_send.at[d], q_recv.at[d], core).wait_recv()
    for copy in local:
        copy.wait()
    for copy in sent:
        copy.wait_send()


def collect(dq, dk, dv):
    dma = pltpu.SemaphoreType.DMA
    hbm = pl.BlockSpec(memory_space=pltpu.HBM)
    piece = (ROWS, 128)
    return pl.pallas_call(
        collect_kernel,
        out_shape=(jax.ShapeDtypeStruct((ROWS, 512), BF16),) * 3,
        in_specs=[hbm] * 3,
        out_specs=(hbm,) * 3,
        scratch_shapes=[
            pltpu.VMEM((2, 4, 2, *piece), BF16),
            pltpu.VMEM((2, 4, 2, *piece), BF16),
            pltpu.VMEM((4, 2, *piece), BF16),
            pltpu.VMEM((4, 2, *piece), BF16),
            pltpu.VMEM((4, 2, *piece), BF16),
            dma((2, 4, 2)), dma((3,)),
            dma((2, 4, 2)), dma((2, 4, 2)),
            dma((4, 2)), dma((4, 2)),
            dma((4, 2)), dma((4, 2)),
            dma((4,)), dma((4,)),
        ],
        compiler_params=pltpu.CompilerParams(
            collective_id=1, has_side_effects=True, vmem_limit_bytes=48 << 20
        ),
        name="collect",
    )(dq, dk, dv)


def store_kernel(*refs):
    ins, outs, sem = refs[:3], refs[3:6], refs[6]
    copies = [pltpu.make_async_copy(a, b, sem.at[i]) for i, (a, b) in enumerate(zip(ins, outs))]
    for copy in copies:
        copy.start()
    for copy in copies:
        copy.wait()


def store(dq, dk, dv):
    anywhere = pl.BlockSpec(memory_space=pl.ANY)
    return pl.pallas_call(
        store_kernel,
        out_shape=(jax.ShapeDtypeStruct((ROWS, 512), BF16),) * 3,
        in_specs=[pl.BlockSpec(memory_space=pltpu.VMEM)] * 3,
        out_specs=(anywhere,) * 3,
        scratch_shapes=[pltpu.SemaphoreType.DMA((3,))],
        name="store",
    )(dq, dk, dv)


def per_device(query_proj, key_proj, value_proj, out_grad, out_weight, block_mask):
    query_proj, key_proj, value_proj, out_grad = [
        pltpu.with_memory_space_constraint(a, pltpu.HBM)
        for a in (query_proj, key_proj, value_proj, out_grad)
    ]
    q, k, v, g = spread(query_proj, key_proj, value_proj, out_grad, out_weight)
    dq, dk, dv = attention(block_mask, q, g, k, v)
    return store(*collect(dq, dk, dv))


def solution(mesh):
    placed = (P("ctx", "tp"), P("ctx", "tp"), P("ctx", "tp"), P("ctx", "tp"), P(None, "tp"), P())
    return jax.shard_map(
        per_device,
        mesh=mesh,
        in_specs=placed,
        out_specs=(P("ctx", "tp"), P("ctx", "tp"), P("ctx", "tp")),
        check_vma=False,
    )
```

```python
import functools

import jax
import jax.numpy as jnp
from jax import lax
from jax.experimental import pallas as pl
from jax.experimental.pallas import tpu as pltpu
from jax.sharding import PartitionSpec as P

MESH = pl.DeviceIdType.MESH
HEAD_DIM = 128
BLOCK = 128
ROWS = 256
NX = 4
NB = 32
NEG_FILL = -1e30
SCALE = HEAD_DIM ** (-0.5)
LOG2E = 1.4426950408889634
BF16 = jnp.bfloat16
F32 = jnp.float32
NT = (((1,), (1,)), ((), ()))


def place():
    ctx, tp = lax.axis_index("ctx"), lax.axis_index("tp")
    return (
        lax.div(ctx, 4),
        lax.rem(lax.div(ctx, 2), 2),
        lax.rem(ctx, 2),
        lax.div(tp, 4),
        lax.rem(tp, 4),
    )


def device(x, z, c, zh, y):
    return {"ctx": x * 4 + z * 2 + c, "tp": zh * 4 + y}


def block_rows(x, z, c):
    return pl.ds(pl.multiple_of((x * 4 + z * 2 + c) * ROWS, ROWS), ROWS)


def head_lanes(h):
    return pl.ds(pl.multiple_of(h * HEAD_DIM, HEAD_DIM), HEAD_DIM)


def remote(src, dst, send, recv, to):
    return pltpu.make_async_remote_copy(
        src_ref=src, dst_ref=dst, send_sem=send, recv_sem=recv, device_id=to, device_id_type=MESH
    )


def pick_blocks(mask, picks, zc):
    down = lax.broadcasted_iota(jnp.int32, (NB, NB), 0)
    across = lax.broadcasted_iota(jnp.int32, (NB, NB), 1)
    upto = jnp.where(across <= down, 1.0, 0.0)
    for i in range(NX):
        first = (i * 4 + zc) * 2
        may = [jnp.where(mask[pl.ds(first + a, 1), :] == 1, 1.0, 0.0) for a in range(2)]
        either = jnp.broadcast_to(jnp.maximum(may[0], may[1]), (8, NB))
        before = lax.dot_general(upto, either, NT, preferred_element_type=F32)[:, 0:1]
        total = jnp.sum(either[0:1], axis=1, keepdims=True).astype(jnp.int32)
        place_of = jnp.sum(
            jnp.where(before.astype(jnp.int32) <= across, 1, 0), axis=0, keepdims=True)
        at = across[0:1]
        chosen = jnp.where((down == place_of) & (at < total), 1.0, 0.0)
        picks[i:i + 1, :] = jnp.where(at < total, place_of, 0)
        for a in range(2):
            held = jnp.dot(jnp.broadcast_to(may[a], (8, NB)), chosen, preferred_element_type=F32)
            picks[4 + 4 * a + i:5 + 4 * a + i, :] = held[0:1].astype(jnp.int32)
        picks[12 + i:13 + i, :] = jnp.broadcast_to(total, (1, NB))


def spread_kernel(
    q_in, k_in, v_in, og_in, w_in, mask_in,
    q_out, k_out, v_out, g_out, picks,
    mask, og, w, own, relay, relay_got, comb, comb_got, direct, direct_got, z_part, z_got, g_part,
    load_sem, local_sem, y_send, y_recv, z_send, z_recv, g_send, g_recv,
    q_send, q_recv, kv_xsend, kv_xrecv, kv_fsend, kv_frecv,
):
    x, z, c, zh, y = place()
    yp, ym, yo = lax.rem(y + 1, 4), lax.rem(y + 3, 4), lax.rem(y + 2, 4)

    def at_x(d):
        return device(lax.rem(x + d, 4), z, c, zh, y)

    core, zpeer = device(x, z, 1 - c, zh, y), device(x, 1 - z, c, zh, y)
    up, down = device(x, z, c, zh, yp), device(x, z, c, zh, ym)
    zfar = device(x, z, c, 1 - zh, y)

    order = [(yo, 0), (yo, 1), (yp, 0), (ym, 1), (yp, 1), (ym, 0), (y, 0), (y, 1)]
    loads = [pltpu.make_async_copy(og_in, og, load_sem.at[8])]
    mask_load = pltpu.make_async_copy(mask_in, mask, load_sem.at[9])
    for i, (yy, zz) in enumerate(order):
        rows = pl.ds(pl.multiple_of((zz * 4 + yy) * 512, 512), 512)
        loads.append(pltpu.make_async_copy(w_in.at[rows], w.at[i], load_sem.at[i]))
    for load in loads:
        load.start()
    mask_load.start()

    barrier = pltpu.get_barrier_semaphore()
    for peer in (at_x(1), at_x(2), at_x(3), core, zpeer, up, down, zfar):
        pl.semaphore_signal(barrier, inc=1, device_id=peer, device_id_type=MESH)
    pl.semaphore_wait(barrier, 8)

    sent = []

    def go(copy):
        copy.start()
        sent.append(copy)

    def project(i):
        loads[1 + i].wait()
        return lax.dot_general(og[...], w[i], NT, preferred_element_type=F32)

    heads = [lax.rem(x + 1 + i, 4) for i in range(4)]

    def y_copy(kind, zz, i, src, dst, to):
        return remote(
            src.at[zz, heads[i]], dst.at[zz, heads[i]],
            y_send.at[kind, zz, i], y_recv.at[kind, zz, i], to,
        )

    loads[0].wait()
    for zz in range(2):
        part = project(zz)
        for h in range(4):
            relay[zz, h] = part[:, h * 128:(h + 1) * 128].astype(BF16)
    relays = [[y_copy(0, zz, i, relay, relay_got, (up, down)[zz]) for i in range(4)] for zz in range(2)]
    for i in range(4):
        for zz in range(2):
            go(relays[zz][i])

    tensors = [(k_in, k_out), (v_in, v_out)]

    def kv_from_x(t, d):
        src, dst = tensors[t]
        return remote(
            src.at[:, head_lanes(lax.rem(x + d, 4))], dst.at[block_rows(x, z, c)],
            kv_xsend.at[t, d], kv_xrecv.at[t, d], at_x(d),
        )

    def kv_wait_x(t, d):
        dst = tensors[t][1].at[block_rows(lax.rem(x + 4 - d, 4), z, c)]
        remote(dst, dst, kv_xsend.at[t, d], kv_xrecv.at[t, d], core).wait_recv()

    def kv_forward(t, d, route):
        xs = lax.rem(x + 4 - d, 4)
        rows = block_rows(xs, z if route < 2 else 1 - z, c)
        dst = tensors[t][1].at[rows]
        src = tensors[t][0].at[:, head_lanes(x)] if (d == 0 and route < 2) else dst
        return remote(
            src, dst, kv_fsend.at[t, d, route], kv_frecv.at[t, d, route], zpeer if route == 1 else core
        )

    def kv_wait(t, d, route):
        xs = lax.rem(x + 4 - d, 4)
        rows = block_rows(xs, z if route == 0 else 1 - z, c if route == 1 else 1 - c)
        dst = tensors[t][1].at[rows]
        remote(dst, dst, kv_fsend.at[t, d, route], kv_frecv.at[t, d, route], core).wait_recv()

    for t in range(2):
        go(kv_forward(t, 0, 1))
    for d in (1, 3, 2):
        for t in range(2):
            go(kv_from_x(t, d))
    for t in range(2):
        go(kv_forward(t, 0, 0))
    local = []
    for t in range(2):
        local.append(pltpu.make_async_copy(
            tensors[t][0].at[:, head_lanes(x)], tensors[t][1].at[block_rows(x, z, c)], local_sem.at[t]))
    q_rows = pl.ds(pl.multiple_of(x * ROWS, ROWS), ROWS)
    local.append(pltpu.make_async_copy(q_in.at[:, head_lanes(x)], q_out.at[q_rows], local_sem.at[2]))
    for copy in local:
        copy.start()
    q_copies = [
        remote(q_in.at[:, head_lanes(lax.rem(x + d, 4))], q_out.at[q_rows], q_send.at[d], q_recv.at[d], at_x(d))
        for d in (1, 2, 3)
    ]

    for i in range(2, 8):
        zz = order[i][1]
        part = project(i)
        for h in range(4):
            piece = part[:, h * 128:(h + 1) * 128]
            if i in (4, 5):
                direct[zz, h] = piece.astype(BF16)
            else:
                own[0 if i < 4 else 1, zz, h] = piece

    def combine(i):
        h = heads[i]
        for zz in range(2):
            relays[zz][i].wait_recv()
            comb[zz, h] = (relay_got[zz, h].astype(F32) + own[0, zz, h]).astype(BF16)
            go(y_copy(1, zz, i, comb, comb_got, (up, down)[zz]))
        for zz in range(2):
            go(y_copy(2, zz, i, direct, direct_got, (down, up)[zz]))

    z_copies = [
        remote(z_part.at[heads[i]], z_got.at[heads[i]], z_send.at[i], z_recv.at[i], zfar) for i in range(4)
    ]

    def finish_y(i):
        h = heads[i]
        for zz in range(2):
            y_copy(1, zz, i, comb, comb_got, up).wait_recv()
            y_copy(2, zz, i, direct, direct_got, up).wait_recv()
        far = own[1, 1 - zh, h] + comb_got[1 - zh, h].astype(F32) + direct_got[1 - zh, h].astype(F32)
        z_part[h] = far.astype(BF16)
        go(z_copies[i])
        own[1, zh, h] = own[1, zh, h] + comb_got[zh, h].astype(F32) + direct_got[zh, h].astype(F32)

    def finish_z(i):
        h = heads[i]
        z_copies[i].wait_recv()
        g_part[h] = (own[1, zh, h] + z_got[h].astype(F32)).astype(BF16)
        if i < 3:
            go(remote(g_part.at[h], g_out.at[q_rows], g_send.at[i], g_recv.at[i], at_x(i + 1)))
        else:
            copy = pltpu.make_async_copy(g_part.at[h], g_out.at[q_rows], local_sem.at[3])
            copy.start()
            local.append(copy)

    def pass_on(d):
        for t in range(2):
            kv_wait_x(t, d)
            go(kv_forward(t, d, 1))
            go(kv_forward(t, d, 0))

    def pass_z(d):
        for t in range(2):
            kv_wait(t, d, 1)
            go(kv_forward(t, d, 2))

    mask_load.wait()
    pick_blocks(mask, picks, z * 2 + c)
    combine(0)
    pass_on(1)
    combine(1)
    pass_on(3)
    for copy in q_copies:
        go(copy)
    combine(2)
    pass_z(0)
    combine(3)
    pass_on(2)
    pass_z(1)
    finish_y(0)
    pass_z(3)
    finish_y(1)
    finish_z(0)
    finish_y(2)
    finish_z(1)
    pass_z(2)
    finish_y(3)
    finish_z(2)
    finish_z(3)

    for d in range(4):
        for t in range(2):
            kv_wait(t, d, 0)
            kv_wait(t, d, 2)
    for copy in q_copies:
        copy.wait_recv()
    for i in range(3):
        rows = pl.ds(pl.multiple_of(lax.rem(x + 3 - i, 4) * ROWS, ROWS), ROWS)
        dst = g_out.at[rows]
        remote(dst, dst, g_send.at[i], g_recv.at[i], core).wait_recv()
    for copy in local:
        copy.wait()
    for copy in sent:
        copy.wait_send()


def spread(q, k, v, og, w, mask):
    dma = pltpu.SemaphoreType.DMA
    hbm = pl.BlockSpec(memory_space=pltpu.HBM)
    vmem = pl.BlockSpec(memory_space=pltpu.VMEM)
    return pl.pallas_call(
        spread_kernel,
        out_shape=(
            jax.ShapeDtypeStruct((NX * ROWS, 128), BF16),
            jax.ShapeDtypeStruct((16 * ROWS, 128), BF16),
            jax.ShapeDtypeStruct((16 * ROWS, 128), BF16),
            jax.ShapeDtypeStruct((NX * ROWS, 128), BF16),
            jax.ShapeDtypeStruct((16, NB), jnp.int32),
        ),
        in_specs=[hbm] * 6,
        out_specs=(hbm,) * 4 + (vmem,),
        scratch_shapes=[
            pltpu.VMEM((NB, NB), jnp.int32),
            pltpu.VMEM((ROWS, 512), BF16),
            pltpu.VMEM((8, 512, 512), BF16),
            pltpu.VMEM((2, 2, 4, ROWS, 128), F32),
            *[pltpu.VMEM((2, 4, ROWS, 128), BF16)] * 6,
            *[pltpu.VMEM((4, ROWS, 128), BF16)] * 3,
            dma((10,)), dma((4,)),
            dma((3, 2, 4)), dma((3, 2, 4)),
            dma((4,)), dma((4,)), dma((3,)), dma((3,)),
            dma((4,)), dma((4,)),
            dma((2, 4)), dma((2, 4)), dma((2, 4, 3)), dma((2, 4, 3)),
        ],
        compiler_params=pltpu.CompilerParams(
            collective_id=0, has_side_effects=True, vmem_limit_bytes=48 << 20
        ),
        name="spread",
    )(q, k, v, og, w, mask)


def attention_kernel(picks, q, g, k, v, dq, dk, dv, s_scr, p_scr, dk_acc, dv_acc):
    dk_acc[...] = jnp.zeros_like(dk_acc)
    dv_acc[...] = jnp.zeros_like(dv_acc)

    def tile(i, carry):
        count = picks[12 + i, 0]
        rest = lax.rem(count, 8)
        wide = lax.div(count, 8) + jnp.where(rest > 4, 1, 0)
        narrow = jnp.where((rest > 0) & (rest <= 4), 1, 0)

        def steps(body, carry):
            carry = lax.fori_loop(0, wide, lambda j, carry: body(8, j * 8, carry), carry)
            return lax.fori_loop(0, narrow, lambda j, carry: body(4, wide * 8, carry), carry)

        q_rows = pl.ds(pl.multiple_of(i * ROWS, ROWS), ROWS)
        q_tile, g_tile = q[q_rows, :], g[q_rows, :]

        def rows_of(n):
            return pl.ds(pl.multiple_of(picks[i, n] * BLOCK, BLOCK), BLOCK)

        def gather(ref, size, base):
            return jnp.concatenate([ref[rows_of(base + n), :] for n in range(size)], axis=0)

        def fold(op, tall):
            return op(tall.reshape(-1, 8, ROWS), axis=0)

        def scores(size, base, top):
            s = lax.dot_general(gather(k, size, base), q_tile, NT, preferred_element_type=F32)
            prob_grad = lax.dot_general(gather(v, size, base), g_tile, NT, preferred_element_type=F32)
            p_scr[pl.ds(base, size)] = prob_grad.reshape(size, BLOCK, ROWS)
            for n in range(size):
                fill = jnp.concatenate(
                    [
                        jnp.full((1, 128), jnp.where(picks[4 + 4 * a + i, base + n] == 1, 0.0, NEG_FILL), F32)
                        for a in range(2)
                    ],
                    axis=1,
                )
                part = s[n * BLOCK:(n + 1) * BLOCK] * (SCALE * LOG2E) + fill
                s_scr[base + n] = part
                top = jnp.maximum(top, fold(jnp.max, part))
            return top

        top = steps(scores, jnp.full((8, ROWS), NEG_FILL, F32))
        top = jnp.max(top, axis=0, keepdims=True)

        def sums(size, base, carry):
            total, weighted = carry
            e = jnp.exp2(s_scr[pl.ds(base, size)] - top)
            s_scr[pl.ds(base, size)] = e
            return total + fold(jnp.sum, e), weighted + fold(jnp.sum, e * p_scr[pl.ds(base, size)])

        zero = jnp.zeros((8, ROWS), F32)
        total, weighted = steps(sums, (zero, zero))
        inverse = 1.0 / jnp.sum(total, axis=0, keepdims=True)
        delta = jnp.sum(weighted, axis=0, keepdims=True) * inverse

        def grads(size, base, dq_acc):
            p = s_scr[pl.ds(base, size)].reshape(size * BLOCK, ROWS) * inverse
            ds = (p * (p_scr[pl.ds(base, size)].reshape(size * BLOCK, ROWS) - delta)).astype(BF16)
            p = p.astype(BF16)
            dv_part = jnp.dot(p, g_tile, preferred_element_type=F32)
            dk_part = jnp.dot(ds, q_tile, preferred_element_type=F32)
            dq_acc = dq_acc + lax.dot_general(
                ds, gather(k, size, base), (((0,), (0,)), ((), ())), preferred_element_type=F32
            )
            for n in range(size):
                rows = rows_of(base + n)
                dk_acc[rows, :] += dk_part[n * BLOCK:(n + 1) * BLOCK]
                dv_acc[rows, :] += dv_part[n * BLOCK:(n + 1) * BLOCK]
            return dq_acc

        dq_acc = steps(grads, jnp.zeros((ROWS, 128), F32))
        dq[q_rows, :] = (dq_acc * SCALE).astype(BF16)
        return carry

    lax.fori_loop(0, NX, tile, 0)
    dk[...] = (dk_acc[...] * SCALE).astype(BF16)
    dv[...] = dv_acc[...].astype(BF16)


def attention(picks, q, g, k, v):
    vmem = pl.BlockSpec(memory_space=pltpu.VMEM)
    return pl.pallas_call(
        attention_kernel,
        out_shape=(
            jax.ShapeDtypeStruct((NX * ROWS, 128), BF16),
            jax.ShapeDtypeStruct((16 * ROWS, 128), BF16),
            jax.ShapeDtypeStruct((16 * ROWS, 128), BF16),
        ),
        in_specs=[pl.BlockSpec(memory_space=pltpu.SMEM)] + [vmem] * 4,
        out_specs=(vmem,) * 3,
        scratch_shapes=[
            pltpu.VMEM((NB, BLOCK, ROWS), F32),
            pltpu.VMEM((NB, BLOCK, ROWS), F32),
            pltpu.VMEM((16 * ROWS, 128), F32),
            pltpu.VMEM((16 * ROWS, 128), F32),
        ],
        compiler_params=pltpu.CompilerParams(vmem_limit_bytes=48 << 20),
        name="attention",
    )(picks, q, g, k, v)


def collect_kernel(
    dq_in, dk_in, dv_in,
    dq_out, dk_out, dv_out,
    own, core_got, z_part, z_got, part,
    load_sem, local_sem, core_send, core_recv, z_send, z_recv, x_send, x_recv, q_send, q_recv,
):
    x, z, c, zh, y = place()

    def at_x(d):
        return device(lax.rem(x + d, 4), z, c, zh, y)

    core, zpeer = device(x, z, 1 - c, zh, y), device(x, 1 - z, c, zh, y)
    tensors = [(dk_in, dk_out), (dv_in, dv_out)]
    order = (1, 3, 2, 0)

    loads = {}
    for far in (1, 0):
        for d in order:
            for t in range(2):
                rows = block_rows(lax.rem(x + d, 4), 1 - z if far else z, c)
                loads[far, d, t] = pltpu.make_async_copy(
                    tensors[t][0].at[rows], own.at[far, d, t], load_sem.at[far, d, t])
                loads[far, d, t].start()

    barrier = pltpu.get_barrier_semaphore()
    for peer in (at_x(1), at_x(2), at_x(3), core, zpeer):
        pl.semaphore_signal(barrier, inc=1, device_id=peer, device_id_type=MESH)
    pl.semaphore_wait(barrier, 5)

    sent = []

    def go(copy):
        copy.start()
        sent.append(copy)

    to_core = {}
    for far in (1, 0):
        for d in order:
            for t in range(2):
                rows = block_rows(lax.rem(x + d, 4), 1 - z if far else z, 1 - c)
                to_core[far, d, t] = remote(
                    tensors[t][0].at[rows], core_got.at[far, d, t],
                    core_send.at[far, d, t], core_recv.at[far, d, t], core)
                go(to_core[far, d, t])

    q_copies = [
        remote(
            dq_in.at[pl.ds(pl.multiple_of(lax.rem(x + d, 4) * ROWS, ROWS), ROWS)],
            dq_out.at[:, head_lanes(x)], q_send.at[d], q_recv.at[d], at_x(d))
        for d in (1, 2, 3)
    ]
    for copy in q_copies:
        go(copy)
    local = [pltpu.make_async_copy(
        dq_in.at[pl.ds(pl.multiple_of(x * ROWS, ROWS), ROWS)], dq_out.at[:, head_lanes(x)], local_sem.at[2])]
    local[0].start()

    to_z = {}
    for d in order:
        for t in range(2):
            loads[1, d, t].wait()
            to_core[1, d, t].wait_recv()
            z_part[d, t] = (own[1, d, t].astype(F32) + core_got[1, d, t].astype(F32)).astype(BF16)
            to_z[d, t] = remote(z_part.at[d, t], z_got.at[d, t], z_send.at[d, t], z_recv.at[d, t], zpeer)
            go(to_z[d, t])
    for d in order:
        for t in range(2):
            loads[0, d, t].wait()
            to_core[0, d, t].wait_recv()
            to_z[d, t].wait_recv()
            part[d, t] = (
                own[0, d, t].astype(F32) + core_got[0, d, t].astype(F32) + z_got[d, t].astype(F32)
            ).astype(BF16)
            dst = tensors[t][1].at[:, head_lanes(x)]
            if d == 0:
                copy = pltpu.make_async_copy(part.at[d, t], dst, local_sem.at[t])
                copy.start()
                local.append(copy)
            else:
                go(remote(part.at[d, t], dst, x_send.at[d, t], x_recv.at[d, t], at_x(d)))

    for d in (1, 2, 3):
        lanes = head_lanes(lax.rem(x + 4 - d, 4))
        for t in range(2):
            dst = tensors[t][1].at[:, lanes]
            remote(dst, dst, x_send.at[d, t], x_recv.at[d, t], core).wait_recv()
        dst = dq_out.at[:, lanes]
        remote(dst, dst, q_send.at[d], q_recv.at[d], core).wait_recv()
    for copy in local:
        copy.wait()
    for copy in sent:
        copy.wait_send()


def collect(dq, dk, dv):
    dma = pltpu.SemaphoreType.DMA
    hbm = pl.BlockSpec(memory_space=pltpu.HBM)
    piece = (ROWS, 128)
    return pl.pallas_call(
        collect_kernel,
        out_shape=(jax.ShapeDtypeStruct((ROWS, 512), BF16),) * 3,
        in_specs=[hbm] * 3,
        out_specs=(hbm,) * 3,
        scratch_shapes=[
            pltpu.VMEM((2, 4, 2, *piece), BF16),
            pltpu.VMEM((2, 4, 2, *piece), BF16),
            pltpu.VMEM((4, 2, *piece), BF16),
            pltpu.VMEM((4, 2, *piece), BF16),
            pltpu.VMEM((4, 2, *piece), BF16),
            dma((2, 4, 2)), dma((3,)),
            dma((2, 4, 2)), dma((2, 4, 2)),
            dma((4, 2)), dma((4, 2)),
            dma((4, 2)), dma((4, 2)),
            dma((4,)), dma((4,)),
        ],
        compiler_params=pltpu.CompilerParams(
            collective_id=1, has_side_effects=True, vmem_limit_bytes=48 << 20
        ),
        name="collect",
    )(dq, dk, dv)


def store_kernel(*refs):
    ins, outs, sem = refs[:3], refs[3:6], refs[6]
    copies = [pltpu.make_async_copy(a, b, sem.at[i]) for i, (a, b) in enumerate(zip(ins, outs))]
    for copy in copies:
        copy.start()
    for copy in copies:
        copy.wait()


def store(dq, dk, dv):
    anywhere = pl.BlockSpec(memory_space=pl.ANY)
    return pl.pallas_call(
        store_kernel,
        out_shape=(jax.ShapeDtypeStruct((ROWS, 512), BF16),) * 3,
        in_specs=[anywhere] * 3,
        out_specs=(anywhere,) * 3,
        scratch_shapes=[pltpu.SemaphoreType.DMA((3,))],
        compiler_params=pltpu.CompilerParams(vmem_limit_bytes=16 << 20),
        name="store",
    )(dq, dk, dv)


def per_device(query_proj, key_proj, value_proj, out_grad, out_weight, block_mask):
    query_proj, key_proj, value_proj, out_grad, block_mask = [
        pltpu.with_memory_space_constraint(a, pltpu.HBM)
        for a in (query_proj, key_proj, value_proj, out_grad, block_mask)
    ]
    q, k, v, g, picks = spread(query_proj, key_proj, value_proj, out_grad, out_weight, block_mask)
    dq, dk, dv = attention(picks, q, g, k, v)
    return store(*collect(dq, dk, dv))


def solution(mesh):
    placed = (P("ctx", "tp"), P("ctx", "tp"), P("ctx", "tp"), P("ctx", "tp"), P(None, "tp"), P())
    return jax.shard_map(
        per_device,
        mesh=mesh,
        in_specs=placed,
        out_specs=(P("ctx", "tp"), P("ctx", "tp"), P("ctx", "tp")),
        check_vma=False,
    )
```

```python
import functools

import jax
import jax.numpy as jnp
from jax import lax
from jax.experimental import pallas as pl
from jax.experimental.pallas import tpu as pltpu
from jax.sharding import PartitionSpec as P

MESH = pl.DeviceIdType.MESH
HEAD_DIM = 128
BLOCK = 128
ROWS = 256
NX = 4
NB = 32
NEG_FILL = -1e30
SCALE = HEAD_DIM ** (-0.5)
LOG2E = 1.4426950408889634
BF16 = jnp.bfloat16
F32 = jnp.float32
NT = (((1,), (1,)), ((), ()))


def place():
    ctx, tp = lax.axis_index("ctx"), lax.axis_index("tp")
    return (
        lax.div(ctx, 4),
        lax.rem(lax.div(ctx, 2), 2),
        lax.rem(ctx, 2),
        lax.div(tp, 4),
        lax.rem(tp, 4),
    )


def device(x, z, c, zh, y):
    return {"ctx": x * 4 + z * 2 + c, "tp": zh * 4 + y}


def block_rows(x, z, c):
    return pl.ds(pl.multiple_of((x * 4 + z * 2 + c) * ROWS, ROWS), ROWS)


def head_lanes(h):
    return pl.ds(pl.multiple_of(h * HEAD_DIM, HEAD_DIM), HEAD_DIM)


def remote(src, dst, send, recv, to):
    return pltpu.make_async_remote_copy(
        src_ref=src, dst_ref=dst, send_sem=send, recv_sem=recv, device_id=to, device_id_type=MESH
    )


def fill_table(mask, fill, zc):
    block = lax.broadcasted_iota(jnp.int32, (NB, NX * ROWS), 0)
    lane = lax.broadcasted_iota(jnp.int32, (NB, NX * ROWS), 1)
    query_block = ((lane >> 8) * 4 + zc) * 2 + ((lane >> 7) & 1)
    own = jnp.where(block == query_block, 1.0, 0.0)
    may = jnp.where(mask[...] == 1, 1.0, 0.0)
    held = lax.dot_general(may, own, (((0,), (0,)), ((), ())), preferred_element_type=F32)
    fill[...] = jnp.where(held > 0.5, 0.0, NEG_FILL)


def unit_scores(k_unit, q, fill, unit, shift):
    s = lax.dot_general(k_unit, q[...], NT, preferred_element_type=F32)
    count = k_unit.shape[0] // BLOCK
    parts = [
        s[a * BLOCK:(a + 1) * BLOCK] * (SCALE * LOG2E) + (fill[pl.ds(unit * count + a, 1), :] - shift)
        for a in range(count)
    ]
    return jnp.concatenate(parts, axis=0)


def start_totals(totals, out_t):
    row = lax.broadcasted_iota(jnp.int32, totals.shape, 0)
    totals[...] = jnp.where(row == 0, NEG_FILL, 0.0)
    out_t[...] = jnp.zeros_like(out_t)


def add_totals(k, v, q, fill, totals, out_t, unit):
    rows = pl.ds(pl.multiple_of(unit * 512, 512), 512)
    s = unit_scores(k[rows, :], q, fill, unit, 0.0)
    old = totals[0:1, :]
    new = jnp.maximum(old, jnp.max(s, axis=0, keepdims=True))
    e = jnp.exp2(s - new)
    keep = jnp.exp2(old - new)
    totals[0:1, :] = new
    totals[1:2, :] = totals[1:2, :] * keep + jnp.sum(e, axis=0, keepdims=True)
    v_t = jnp.concatenate([v[rows, :].T, jnp.ones((16, 512), BF16)], axis=0)
    out_t[...] = out_t[...] * keep + jnp.dot(v_t, e.astype(BF16), preferred_element_type=F32)


def end_totals(totals, out_t, log_total, mean_t):
    log_total[...] = totals[0:1, :] + jnp.log(totals[1:2, :]) * LOG2E
    mean_t[...] = out_t[0:128, :] * (1.0 / out_t[128:129, :])


def spread_kernel(
    q_in, k_in, v_in, og_in, w_in, mask_in,
    q_out, k_out, v_out, g_out, fill, log_total, mean_t,
    mask, totals, out_t, og, w, own, relay, relay_got, comb, comb_got, direct, direct_got, z_part, z_got, g_part,
    load_sem, local_sem, y_send, y_recv, z_send, z_recv, g_send, g_recv,
    q_send, q_recv, kv_xsend, kv_xrecv, kv_fsend, kv_frecv,
):
    x, z, c, zh, y = place()
    yp, ym, yo = lax.rem(y + 1, 4), lax.rem(y + 3, 4), lax.rem(y + 2, 4)

    def at_x(d):
        return device(lax.rem(x + d, 4), z, c, zh, y)

    core, zpeer = device(x, z, 1 - c, zh, y), device(x, 1 - z, c, zh, y)
    up, down = device(x, z, c, zh, yp), device(x, z, c, zh, ym)
    zfar = device(x, z, c, 1 - zh, y)

    order = [(yo, 0), (yo, 1), (yp, 0), (ym, 1), (yp, 1), (ym, 0), (y, 0), (y, 1)]
    loads = [pltpu.make_async_copy(og_in, og, load_sem.at[8])]
    mask_load = pltpu.make_async_copy(mask_in, mask, load_sem.at[9])
    for i, (yy, zz) in enumerate(order):
        rows = pl.ds(pl.multiple_of((zz * 4 + yy) * 512, 512), 512)
        loads.append(pltpu.make_async_copy(w_in.at[rows], w.at[i], load_sem.at[i]))
    for load in loads:
        load.start()
    mask_load.start()

    barrier = pltpu.get_barrier_semaphore()
    for peer in (at_x(1), at_x(2), at_x(3), core, zpeer, up, down, zfar):
        pl.semaphore_signal(barrier, inc=1, device_id=peer, device_id_type=MESH)
    pl.semaphore_wait(barrier, 8)

    sent = []

    def go(copy):
        copy.start()
        sent.append(copy)

    def project(i):
        loads[1 + i].wait()
        return lax.dot_general(og[...], w[i], NT, preferred_element_type=F32)

    heads = [lax.rem(x + 1 + i, 4) for i in range(4)]

    def y_copy(kind, zz, i, src, dst, to):
        return remote(
            src.at[zz, heads[i]], dst.at[zz, heads[i]],
            y_send.at[kind, zz, i], y_recv.at[kind, zz, i], to,
        )

    turns = [[y_copy(0, zz, i, relay, relay_got, (up, down)[zz]) for zz in range(2)] for i in range(4)]
    for i in range(4):
        turns.append([y_copy(1, zz, i, comb, comb_got, (up, down)[zz]) for zz in range(2)])
        turns.append([y_copy(2, zz, i, direct, direct_got, (down, up)[zz]) for zz in range(2)])

    def turn(n):
        for copy in turns[n]:
            go(copy)

    loads[0].wait()
    for zz in range(2):
        part = project(zz)
        for h in range(4):
            relay[zz, h] = part[:, h * 128:(h + 1) * 128].astype(BF16)
    for n in range(4):
        turn(n)

    tensors = [(k_in, k_out), (v_in, v_out)]

    def kv_from_x(t, d):
        src, dst = tensors[t]
        return remote(
            src.at[:, head_lanes(lax.rem(x + d, 4))], dst.at[block_rows(x, z, c)],
            kv_xsend.at[t, d], kv_xrecv.at[t, d], at_x(d),
        )

    def kv_wait_x(t, d):
        dst = tensors[t][1].at[block_rows(lax.rem(x + 4 - d, 4), z, c)]
        remote(dst, dst, kv_xsend.at[t, d], kv_xrecv.at[t, d], core).wait_recv()

    def kv_forward(t, d, route):
        xs = lax.rem(x + 4 - d, 4)
        rows = block_rows(xs, z if route < 2 else 1 - z, c)
        dst = tensors[t][1].at[rows]
        src = tensors[t][0].at[:, head_lanes(x)] if (d == 0 and route < 2) else dst
        return remote(
            src, dst, kv_fsend.at[t, d, route], kv_frecv.at[t, d, route], zpeer if route == 1 else core
        )

    def kv_wait(t, d, route):
        xs = lax.rem(x + 4 - d, 4)
        rows = block_rows(xs, z if route == 0 else 1 - z, c if route == 1 else 1 - c)
        dst = tensors[t][1].at[rows]
        remote(dst, dst, kv_fsend.at[t, d, route], kv_frecv.at[t, d, route], core).wait_recv()

    for t in range(2):
        go(kv_forward(t, 0, 1))
    for d in (1, 3, 2):
        for t in range(2):
            go(kv_from_x(t, d))
    for t in range(2):
        go(kv_forward(t, 0, 0))
    local = []
    for t in range(2):
        local.append(pltpu.make_async_copy(
            tensors[t][0].at[:, head_lanes(x)], tensors[t][1].at[block_rows(x, z, c)], local_sem.at[t]))
    q_rows = pl.ds(pl.multiple_of(x * ROWS, ROWS), ROWS)
    local.append(pltpu.make_async_copy(q_in.at[:, head_lanes(x)], q_out.at[q_rows], local_sem.at[2]))
    for copy in local:
        copy.start()
    q_copies = [
        remote(q_in.at[:, head_lanes(lax.rem(x + d, 4))], q_out.at[q_rows], q_send.at[d], q_recv.at[d], at_x(d))
        for d in (1, 2, 3)
    ]

    for i in range(2, 8):
        zz = order[i][1]
        part = project(i)
        for h in range(4):
            piece = part[:, h * 128:(h + 1) * 128]
            if i in (4, 5):
                direct[zz, h] = piece.astype(BF16)
            else:
                own[0 if i < 4 else 1, zz, h] = piece

    def combine(i):
        h = heads[i]
        for zz in range(2):
            turns[i][zz].wait_recv()
            comb[zz, h] = (relay_got[zz, h].astype(F32) + own[0, zz, h]).astype(BF16)

    z_copies = [
        remote(z_part.at[heads[i]], z_got.at[heads[i]], z_send.at[i], z_recv.at[i], zfar) for i in range(4)
    ]

    def finish_y(i):
        h = heads[i]
        for zz in range(2):
            y_copy(1, zz, i, comb, comb_got, up).wait_recv()
            y_copy(2, zz, i, direct, direct_got, up).wait_recv()
        far = own[1, 1 - zh, h] + comb_got[1 - zh, h].astype(F32) + direct_got[1 - zh, h].astype(F32)
        z_part[h] = far.astype(BF16)
        go(z_copies[i])
        own[1, zh, h] = own[1, zh, h] + comb_got[zh, h].astype(F32) + direct_got[zh, h].astype(F32)

    def finish_z(i):
        h = heads[i]
        z_copies[i].wait_recv()
        g_part[h] = (own[1, zh, h] + z_got[h].astype(F32)).astype(BF16)
        if i < 3:
            go(remote(g_part.at[h], g_out.at[q_rows], g_send.at[i], g_recv.at[i], at_x(i + 1)))
        else:
            copy = pltpu.make_async_copy(g_part.at[h], g_out.at[q_rows], local_sem.at[3])
            copy.start()
            local.append(copy)

    def pass_on(d):
        for t in range(2):
            kv_wait_x(t, d)
            go(kv_forward(t, d, 1))
            go(kv_forward(t, d, 0))

    def pass_z(d):
        for t in range(2):
            kv_wait(t, d, 1)
            go(kv_forward(t, d, 2))

    for copy in q_copies:
        go(copy)
    mask_load.wait()
    fill_table(mask, fill, z * 2 + c)
    start_totals(totals, out_t)
    for i in range(4):
        combine(i)
        turn(4 + 2 * i)
        turn(5 + 2 * i)
        if i < 3:
            pass_on((1, 3, 2)[i])

    def add_units(distances, zz):
        def one(i, carry):
            d = distances[0] + i * (distances[-1] - distances[0])
            add_totals(k_out, v_out, q_out, fill, totals, out_t, lax.rem(x + 8 - d, 4) * 2 + zz)
            return carry

        lax.fori_loop(0, len(distances), one, 0)

    def await_core(d, route):
        for t in range(2):
            kv_wait(t, d, route)

    for copy in q_copies:
        copy.wait_recv()
    for copy in local:
        copy.wait()
    local.clear()
    await_core(0, 0)
    await_core(1, 0)
    add_units((0, 1), z)
    finish_y(0)
    pass_z(0)
    await_core(3, 0)
    await_core(2, 0)
    add_units((3, 2), z)
    pass_z(1)
    finish_y(1)
    finish_z(0)
    await_core(0, 2)
    await_core(1, 2)
    add_units((0, 1), 1 - z)
    pass_z(3)
    pass_z(2)
    finish_y(2)
    finish_z(1)
    await_core(3, 2)
    await_core(2, 2)
    add_units((3, 2), 1 - z)
    end_totals(totals, out_t, log_total, mean_t)
    finish_y(3)
    finish_z(2)
    finish_z(3)

    for i in range(3):
        rows = pl.ds(pl.multiple_of(lax.rem(x + 3 - i, 4) * ROWS, ROWS), ROWS)
        dst = g_out.at[rows]
        remote(dst, dst, g_send.at[i], g_recv.at[i], core).wait_recv()
    for copy in local:
        copy.wait()
    for copy in sent:
        copy.wait_send()


def spread(q, k, v, og, w, mask):
    dma = pltpu.SemaphoreType.DMA
    hbm = pl.BlockSpec(memory_space=pltpu.HBM)
    vmem = pl.BlockSpec(memory_space=pltpu.VMEM)
    return pl.pallas_call(
        spread_kernel,
        out_shape=(
            jax.ShapeDtypeStruct((NX * ROWS, 128), BF16),
            jax.ShapeDtypeStruct((16 * ROWS, 128), BF16),
            jax.ShapeDtypeStruct((16 * ROWS, 128), BF16),
            jax.ShapeDtypeStruct((NX * ROWS, 128), BF16),
            jax.ShapeDtypeStruct((NB, NX * ROWS), F32),
            jax.ShapeDtypeStruct((1, NX * ROWS), F32),
            jax.ShapeDtypeStruct((128, NX * ROWS), F32),
        ),
        in_specs=[hbm] * 6,
        out_specs=(vmem,) * 7,
        scratch_shapes=[
            pltpu.VMEM((NB, NB), jnp.int32),
            pltpu.VMEM((8, NX * ROWS), F32),
            pltpu.VMEM((144, NX * ROWS), F32),
            pltpu.VMEM((ROWS, 512), BF16),
            pltpu.VMEM((8, 512, 512), BF16),
            pltpu.VMEM((2, 2, 4, ROWS, 128), F32),
            *[pltpu.VMEM((2, 4, ROWS, 128), BF16)] * 6,
            *[pltpu.VMEM((4, ROWS, 128), BF16)] * 3,
            dma((10,)), dma((4,)),
            dma((3, 2, 4)), dma((3, 2, 4)),
            dma((4,)), dma((4,)), dma((3,)), dma((3,)),
            dma((4,)), dma((4,)),
            dma((2, 4)), dma((2, 4)), dma((2, 4, 3)), dma((2, 4, 3)),
        ],
        compiler_params=pltpu.CompilerParams(
            collective_id=0, has_side_effects=True, vmem_limit_bytes=48 << 20
        ),
        name="spread",
    )(q, k, v, og, w, mask)


def backward_kernel(
    q, g, k, v, fill, log_total, mean_t,
    dq_out, dk_out, dv_out,
    delta, dq_t, dq_part,
    held, core_got, z_part, z_got, part,
    local_sem, core_send, core_recv, z_send, z_recv, x_send, x_recv, q_send, q_recv,
):
    x, z, c, zh, y = place()

    def at_x(d):
        return device(lax.rem(x + d, 4), z, c, zh, y)

    core, zpeer = device(x, z, 1 - c, zh, y), device(x, 1 - z, c, zh, y)
    outs = (dk_out, dv_out)

    barrier = pltpu.get_barrier_semaphore()
    for peer in (at_x(1), at_x(2), at_x(3), core, zpeer):
        pl.semaphore_signal(barrier, inc=1, device_id=peer, device_id_type=MESH)

    delta[...] = jnp.sum(mean_t[...] * g[...].T.astype(F32), axis=0, keepdims=True)
    dq_t[...] = jnp.zeros_like(dq_t)

    pl.semaphore_wait(barrier, 5)

    def unit_grads(unit, slot, mine):
        rows = pl.ds(pl.multiple_of(unit * ROWS, ROWS), ROWS)
        k_unit = k[rows, :]
        p = jnp.exp2(unit_scores(k_unit, q, fill, unit, log_total[...]))
        prob_grad = lax.dot_general(v[rows, :], g[...], NT, preferred_element_type=F32)
        ds = (p * (prob_grad - delta[...])).astype(BF16)
        held[slot, mine, 1] = jnp.dot(p.astype(BF16), g[...], preferred_element_type=F32).astype(BF16)
        held[slot, mine, 0] = (jnp.dot(ds, q[...], preferred_element_type=F32) * SCALE).astype(BF16)
        dq_t[...] += jnp.dot(k_unit.T, ds, preferred_element_type=F32)

    def core_copy(slot, t):
        return remote(
            held.at[slot, 0, t], core_got.at[slot, t], core_send.at[slot, t], core_recv.at[slot, t], core)

    def z_copy(i, t):
        return remote(z_part.at[i, t], z_got.at[i, t], z_send.at[i, t], z_recv.at[i, t], zpeer)

    def x_copy(i, t):
        return remote(
            part.at[i, t], outs[t].at[:, head_lanes(x)], x_send.at[i, t], x_recv.at[i, t], at_x(i + 1))

    def summed(slot, t):
        core_copy(slot, t).wait_recv()
        return held[slot, 1, t].astype(F32) + core_got[slot, t].astype(F32)

    def finish(i):
        for t in range(2):
            mine = summed(4 + i, t)
            z_copy(i, t).wait_recv()
            part[i, t] = (mine + z_got[i, t].astype(F32)).astype(BF16)

    def step(slot, carry):
        xx = lax.rem(x + 1 + slot, 4)
        zz = jnp.where(slot < 4, 1 - z, z)

        def half(mine, carry):
            unit_grads(xx * 4 + zz * 2 + jnp.where(mine == 0, 1 - c, c), slot, mine)

            @pl.when(mine == 0)
            def _():
                for t in range(2):
                    core_copy(slot, t).start()

            return carry

        lax.fori_loop(0, 2, half, 0)

        @pl.when(slot < 4)
        def _():
            for t in range(2):
                z_part[slot, t] = summed(slot, t).astype(BF16)
                z_copy(slot, t).start()

        @pl.when((slot >= 4) & (slot < 7))
        def _():
            finish(slot - 4)
            for t in range(2):
                x_copy(slot - 4, t).start()

        return carry

    lax.fori_loop(0, 8, step, 0)
    dq_part[...] = (dq_t[...] * SCALE).T.astype(BF16)

    def q_rows(xx):
        return pl.ds(pl.multiple_of(xx * ROWS, ROWS), ROWS)

    q_copies = [
        remote(
            dq_part.at[q_rows(lax.rem(x + d, 4))], dq_out.at[:, head_lanes(x)],
            q_send.at[d], q_recv.at[d], at_x(d))
        for d in (1, 2, 3)
    ]
    for copy in q_copies:
        copy.start()
    q_local = pltpu.make_async_copy(dq_part.at[q_rows(x)], dq_out.at[:, head_lanes(x)], local_sem.at[2])
    q_local.start()
    finish(3)
    for t in range(2):
        pltpu.make_async_copy(part.at[3, t], outs[t].at[:, head_lanes(x)], local_sem.at[t]).start()

    for i in range(3):
        lanes = head_lanes(lax.rem(x + 3 - i, 4))
        for t in range(2):
            dst = outs[t].at[:, lanes]
            remote(dst, dst, x_send.at[i, t], x_recv.at[i, t], core).wait_recv()
        dst = dq_out.at[:, lanes]
        remote(dst, dst, q_send.at[i + 1], q_recv.at[i + 1], core).wait_recv()
    q_local.wait()
    for t in range(2):
        pltpu.make_async_copy(part.at[3, t], outs[t].at[:, head_lanes(x)], local_sem.at[t]).wait()
        for i in range(3):
            x_copy(i, t).wait_send()
        for i in range(4):
            z_copy(i, t).wait_send()
        for slot in range(8):
            core_copy(slot, t).wait_send()
    for copy in q_copies:
        copy.wait_send()


def backward(*operands):
    dma = pltpu.SemaphoreType.DMA
    hbm = pl.BlockSpec(memory_space=pltpu.HBM)
    vmem = pl.BlockSpec(memory_space=pltpu.VMEM)
    piece = (2, ROWS, 128)
    lanes = NX * ROWS
    return pl.pallas_call(
        backward_kernel,
        out_shape=(jax.ShapeDtypeStruct((ROWS, 512), BF16),) * 3,
        in_specs=[vmem] * 7,
        out_specs=(hbm,) * 3,
        scratch_shapes=[
            pltpu.VMEM((1, lanes), F32),
            pltpu.VMEM((128, lanes), F32),
            pltpu.VMEM((lanes, 128), BF16),
            pltpu.VMEM((8, 2, *piece), BF16),
            pltpu.VMEM((8, *piece), BF16),
            *[pltpu.VMEM((4, *piece), BF16)] * 3,
            dma((3,)),
            dma((8, 2)), dma((8, 2)),
            dma((4, 2)), dma((4, 2)),
            dma((3, 2)), dma((3, 2)),
            dma((4,)), dma((4,)),
        ],
        compiler_params=pltpu.CompilerParams(
            collective_id=1, has_side_effects=True, vmem_limit_bytes=48 << 20
        ),
        name="backward",
    )(*operands)


def store_kernel(*refs):
    ins, outs, sem = refs[:3], refs[3:6], refs[6]
    copies = [pltpu.make_async_copy(a, b, sem.at[i]) for i, (a, b) in enumerate(zip(ins, outs))]
    for copy in copies:
        copy.start()
    for copy in copies:
        copy.wait()


def store(dq, dk, dv):
    anywhere = pl.BlockSpec(memory_space=pl.ANY)
    return pl.pallas_call(
        store_kernel,
        out_shape=(jax.ShapeDtypeStruct((ROWS, 512), BF16),) * 3,
        in_specs=[anywhere] * 3,
        out_specs=(anywhere,) * 3,
        scratch_shapes=[pltpu.SemaphoreType.DMA((3,))],
        compiler_params=pltpu.CompilerParams(vmem_limit_bytes=16 << 20),
        name="store",
    )(dq, dk, dv)


def per_device(query_proj, key_proj, value_proj, out_grad, out_weight, block_mask):
    query_proj, key_proj, value_proj, out_grad, block_mask = [
        pltpu.with_memory_space_constraint(a, pltpu.HBM)
        for a in (query_proj, key_proj, value_proj, out_grad, block_mask)
    ]
    q, k, v, g, fill, log_total, mean_t = spread(
        query_proj, key_proj, value_proj, out_grad, out_weight, block_mask
    )
    return store(*backward(q, g, k, v, fill, log_total, mean_t))


def solution(mesh):
    placed = (P("ctx", "tp"), P("ctx", "tp"), P("ctx", "tp"), P("ctx", "tp"), P(None, "tp"), P())
    return jax.shard_map(
        per_device,
        mesh=mesh,
        in_specs=placed,
        out_specs=(P("ctx", "tp"), P("ctx", "tp"), P("ctx", "tp")),
        check_vma=False,
    )
```

```python
import functools

import jax
import jax.numpy as jnp
from jax import lax
from jax.experimental import pallas as pl
from jax.experimental.pallas import tpu as pltpu
from jax.sharding import PartitionSpec as P

MESH = pl.DeviceIdType.MESH
HEAD_DIM = 128
BLOCK = 128
ROWS = 256
NX = 4
NB = 32
NEG_FILL = -1e30
SCALE = HEAD_DIM ** (-0.5)
LOG2E = 1.4426950408889634
BF16 = jnp.bfloat16
F32 = jnp.float32
NT = (((1,), (1,)), ((), ()))


def place():
    ctx, tp = lax.axis_index("ctx"), lax.axis_index("tp")
    return (
        lax.div(ctx, 4),
        lax.rem(lax.div(ctx, 2), 2),
        lax.rem(ctx, 2),
        lax.div(tp, 4),
        lax.rem(tp, 4),
    )


def device(x, z, c, zh, y):
    return {"ctx": x * 4 + z * 2 + c, "tp": zh * 4 + y}


def block_rows(x, z, c):
    return pl.ds(pl.multiple_of((x * 4 + z * 2 + c) * ROWS, ROWS), ROWS)


def head_lanes(h):
    return pl.ds(pl.multiple_of(h * HEAD_DIM, HEAD_DIM), HEAD_DIM)


def remote(src, dst, send, recv, to):
    return pltpu.make_async_remote_copy(
        src_ref=src, dst_ref=dst, send_sem=send, recv_sem=recv, device_id=to, device_id_type=MESH
    )


def fill_table(mask, fill, zc):
    block = lax.broadcasted_iota(jnp.int32, (NB, NX * ROWS), 0)
    lane = lax.broadcasted_iota(jnp.int32, (NB, NX * ROWS), 1)
    query_block = ((lane >> 8) * 4 + zc) * 2 + ((lane >> 7) & 1)
    own = jnp.where(block == query_block, 1.0, 0.0)
    may = jnp.where(mask[...] == 1, 1.0, 0.0)
    held = lax.dot_general(may, own, (((0,), (0,)), ((), ())), preferred_element_type=F32)
    fill[...] = jnp.where(held > 0.5, 0.0, NEG_FILL)


def unit_scores(k_unit, q, fill, unit, shift):
    s = lax.dot_general(k_unit, q[...], NT, preferred_element_type=F32)
    count = k_unit.shape[0] // BLOCK
    parts = [
        s[a * BLOCK:(a + 1) * BLOCK] * (SCALE * LOG2E) + (fill[pl.ds(unit * count + a, 1), :] - shift)
        for a in range(count)
    ]
    return jnp.concatenate(parts, axis=0)


def start_totals(totals, out_t):
    row = lax.broadcasted_iota(jnp.int32, totals.shape, 0)
    totals[...] = jnp.where(row == 0, NEG_FILL, 0.0)
    out_t[...] = jnp.zeros_like(out_t)


def add_totals(k, v, q, fill, totals, out_t, unit):
    rows = pl.ds(pl.multiple_of(unit * 512, 512), 512)
    s = unit_scores(k[rows, :], q, fill, unit, 0.0)
    old = totals[0:1, :]
    new = jnp.maximum(old, jnp.max(s, axis=0, keepdims=True))
    e = jnp.exp2(s - new)
    keep = jnp.exp2(old - new)
    totals[0:1, :] = new
    totals[1:2, :] = totals[1:2, :] * keep + jnp.sum(e, axis=0, keepdims=True)
    v_t = jnp.concatenate([v[rows, :].T, jnp.ones((16, 512), BF16)], axis=0)
    out_t[...] = out_t[...] * keep + jnp.dot(v_t, e.astype(BF16), preferred_element_type=F32)


def end_totals(totals, out_t, log_total, mean_t):
    log_total[...] = totals[0:1, :] + jnp.log(totals[1:2, :]) * LOG2E
    mean_t[...] = out_t[0:128, :] * (1.0 / out_t[128:129, :])


def spread_kernel(
    q_in, k_in, v_in, og_in, w_in, mask_in,
    q_out, k_out, v_out, g_out, fill, log_total, mean_t,
    mask, totals, out_t, og, w, own, relay, relay_got, comb, comb_got, direct, direct_got, z_part, z_got, g_part,
    load_sem, local_sem, y_send, y_recv, z_send, z_recv, g_send, g_recv,
    q_send, q_recv, kv_xsend, kv_xrecv, kv_fsend, kv_frecv,
):
    x, z, c, zh, y = place()
    yp, ym, yo = lax.rem(y + 1, 4), lax.rem(y + 3, 4), lax.rem(y + 2, 4)

    def at_x(d):
        return device(lax.rem(x + d, 4), z, c, zh, y)

    core, zpeer = device(x, z, 1 - c, zh, y), device(x, 1 - z, c, zh, y)
    up, down = device(x, z, c, zh, yp), device(x, z, c, zh, ym)
    zfar = device(x, z, c, 1 - zh, y)

    order = [(yo, 0), (yo, 1), (yp, 0), (ym, 1), (yp, 1), (ym, 0), (y, 0), (y, 1)]
    loads = [pltpu.make_async_copy(og_in, og, load_sem.at[8])]
    mask_load = pltpu.make_async_copy(mask_in, mask, load_sem.at[9])
    for i, (yy, zz) in enumerate(order):
        rows = pl.ds(pl.multiple_of((zz * 4 + yy) * 512, 512), 512)
        loads.append(pltpu.make_async_copy(w_in.at[rows], w.at[i], load_sem.at[i]))
    for load in loads:
        load.start()
    mask_load.start()

    barrier = pltpu.get_barrier_semaphore()
    for peer in (at_x(1), at_x(2), at_x(3), core, zpeer, up, down, zfar):
        pl.semaphore_signal(barrier, inc=1, device_id=peer, device_id_type=MESH)
    pl.semaphore_wait(barrier, 8)

    sent = []

    def go(copy):
        copy.start()
        sent.append(copy)

    def project(i):
        loads[1 + i].wait()
        return lax.dot_general(og[...], w[i], NT, preferred_element_type=F32)

    heads = [lax.rem(x + 1 + i, 4) for i in range(4)]

    def y_copy(kind, zz, i, src, dst, to):
        return remote(
            src.at[zz, heads[i]], dst.at[zz, heads[i]],
            y_send.at[kind, zz, i], y_recv.at[kind, zz, i], to,
        )

    turns = [[y_copy(0, zz, i, relay, relay_got, (up, down)[zz]) for zz in range(2)] for i in range(4)]
    for i in range(4):
        turns.append([y_copy(1, zz, i, comb, comb_got, (up, down)[zz]) for zz in range(2)])
        turns.append([y_copy(2, zz, i, direct, direct_got, (down, up)[zz]) for zz in range(2)])

    def turn(n):
        for copy in turns[n]:
            go(copy)

    loads[0].wait()
    for zz in range(2):
        part = project(zz)
        for h in range(4):
            relay[zz, h] = part[:, h * 128:(h + 1) * 128].astype(BF16)
    for n in range(4):
        turn(n)

    tensors = [(k_in, k_out), (v_in, v_out)]

    def kv_from_x(t, d):
        src, dst = tensors[t]
        return remote(
            src.at[:, head_lanes(lax.rem(x + d, 4))], dst.at[block_rows(x, z, c)],
            kv_xsend.at[t, d], kv_xrecv.at[t, d], at_x(d),
        )

    def kv_wait_x(t, d):
        dst = tensors[t][1].at[block_rows(lax.rem(x + 4 - d, 4), z, c)]
        remote(dst, dst, kv_xsend.at[t, d], kv_xrecv.at[t, d], core).wait_recv()

    def kv_forward(t, d, route):
        xs = lax.rem(x + 4 - d, 4)
        rows = block_rows(xs, z if route < 2 else 1 - z, c)
        dst = tensors[t][1].at[rows]
        src = tensors[t][0].at[:, head_lanes(x)] if (d == 0 and route < 2) else dst
        return remote(
            src, dst, kv_fsend.at[t, d, route], kv_frecv.at[t, d, route], zpeer if route == 1 else core
        )

    def kv_wait(t, d, route):
        xs = lax.rem(x + 4 - d, 4)
        rows = block_rows(xs, z if route == 0 else 1 - z, c if route == 1 else 1 - c)
        dst = tensors[t][1].at[rows]
        remote(dst, dst, kv_fsend.at[t, d, route], kv_frecv.at[t, d, route], core).wait_recv()

    for t in range(2):
        go(kv_forward(t, 0, 1))
    for d in (1, 3, 2):
        for t in range(2):
            go(kv_from_x(t, d))
    for t in range(2):
        go(kv_forward(t, 0, 0))
    local = []
    for t in range(2):
        local.append(pltpu.make_async_copy(
            tensors[t][0].at[:, head_lanes(x)], tensors[t][1].at[block_rows(x, z, c)], local_sem.at[t]))
    q_rows = pl.ds(pl.multiple_of(x * ROWS, ROWS), ROWS)
    local.append(pltpu.make_async_copy(q_in.at[:, head_lanes(x)], q_out.at[q_rows], local_sem.at[2]))
    for copy in local:
        copy.start()
    q_copies = [
        remote(q_in.at[:, head_lanes(lax.rem(x + d, 4))], q_out.at[q_rows], q_send.at[d], q_recv.at[d], at_x(d))
        for d in (1, 2, 3)
    ]

    for i in range(2, 8):
        zz = order[i][1]
        part = project(i)
        for h in range(4):
            piece = part[:, h * 128:(h + 1) * 128]
            if i in (4, 5):
                direct[zz, h] = piece.astype(BF16)
            else:
                own[0 if i < 4 else 1, zz, h] = piece

    def combine(i):
        h = heads[i]
        for zz in range(2):
            turns[i][zz].wait_recv()
            comb[zz, h] = (relay_got[zz, h].astype(F32) + own[0, zz, h]).astype(BF16)

    z_copies = [
        remote(z_part.at[heads[i]], z_got.at[heads[i]], z_send.at[i], z_recv.at[i], zfar) for i in range(4)
    ]

    def finish_y(i):
        h = heads[i]
        for zz in range(2):
            y_copy(1, zz, i, comb, comb_got, up).wait_recv()
            y_copy(2, zz, i, direct, direct_got, up).wait_recv()
        far = own[1, 1 - zh, h] + comb_got[1 - zh, h].astype(F32) + direct_got[1 - zh, h].astype(F32)
        z_part[h] = far.astype(BF16)
        go(z_copies[i])
        own[1, zh, h] = own[1, zh, h] + comb_got[zh, h].astype(F32) + direct_got[zh, h].astype(F32)

    def finish_z(i):
        h = heads[i]
        z_copies[i].wait_recv()
        g_part[h] = (own[1, zh, h] + z_got[h].astype(F32)).astype(BF16)
        if i < 3:
            go(remote(g_part.at[h], g_out.at[q_rows], g_send.at[i], g_recv.at[i], at_x(i + 1)))
        else:
            copy = pltpu.make_async_copy(g_part.at[h], g_out.at[q_rows], local_sem.at[3])
            copy.start()
            local.append(copy)

    def pass_on(d):
        for t in range(2):
            kv_wait_x(t, d)
            go(kv_forward(t, d, 1))
            go(kv_forward(t, d, 0))

    def pass_z(d):
        for t in range(2):
            kv_wait(t, d, 1)
            go(kv_forward(t, d, 2))

    for copy in q_copies:
        go(copy)
    mask_load.wait()
    fill_table(mask, fill, z * 2 + c)
    start_totals(totals, out_t)
    for i in range(4):
        combine(i)
        turn(4 + 2 * i)
        turn(5 + 2 * i)
        if i < 3:
            pass_on((1, 3, 2)[i])

    def add_units(distances, zz):
        def one(i, carry):
            d = distances[0] + i * (distances[-1] - distances[0])
            add_totals(k_out, v_out, q_out, fill, totals, out_t, lax.rem(x + 8 - d, 4) * 2 + zz)
            return carry

        lax.fori_loop(0, len(distances), one, 0, unroll=True)

    def await_core(d, route):
        for t in range(2):
            kv_wait(t, d, route)

    for copy in q_copies:
        copy.wait_recv()
    for copy in local:
        copy.wait()
    local.clear()
    await_core(0, 0)
    await_core(1, 0)
    add_units((0, 1), z)
    finish_y(0)
    pass_z(0)
    await_core(3, 0)
    await_core(2, 0)
    add_units((3, 2), z)
    pass_z(1)
    finish_y(1)
    finish_z(0)
    await_core(0, 2)
    await_core(1, 2)
    add_units((0, 1), 1 - z)
    pass_z(3)
    pass_z(2)
    finish_y(2)
    finish_z(1)
    await_core(3, 2)
    await_core(2, 2)
    add_units((3, 2), 1 - z)
    end_totals(totals, out_t, log_total, mean_t)
    finish_y(3)
    finish_z(2)
    finish_z(3)

    for i in range(3):
        rows = pl.ds(pl.multiple_of(lax.rem(x + 3 - i, 4) * ROWS, ROWS), ROWS)
        dst = g_out.at[rows]
        remote(dst, dst, g_send.at[i], g_recv.at[i], core).wait_recv()
    for copy in local:
        copy.wait()
    for copy in sent:
        copy.wait_send()


def spread(q, k, v, og, w, mask):
    dma = pltpu.SemaphoreType.DMA
    hbm = pl.BlockSpec(memory_space=pltpu.HBM)
    vmem = pl.BlockSpec(memory_space=pltpu.VMEM)
    return pl.pallas_call(
        spread_kernel,
        out_shape=(
            jax.ShapeDtypeStruct((NX * ROWS, 128), BF16),
            jax.ShapeDtypeStruct((16 * ROWS, 128), BF16),
            jax.ShapeDtypeStruct((16 * ROWS, 128), BF16),
            jax.ShapeDtypeStruct((NX * ROWS, 128), BF16),
            jax.ShapeDtypeStruct((NB, NX * ROWS), F32),
            jax.ShapeDtypeStruct((1, NX * ROWS), F32),
            jax.ShapeDtypeStruct((128, NX * ROWS), F32),
        ),
        in_specs=[hbm] * 6,
        out_specs=(vmem,) * 7,
        scratch_shapes=[
            pltpu.VMEM((NB, NB), jnp.int32),
            pltpu.VMEM((8, NX * ROWS), F32),
            pltpu.VMEM((144, NX * ROWS), F32),
            pltpu.VMEM((ROWS, 512), BF16),
            pltpu.VMEM((8, 512, 512), BF16),
            pltpu.VMEM((2, 2, 4, ROWS, 128), F32),
            *[pltpu.VMEM((2, 4, ROWS, 128), BF16)] * 6,
            *[pltpu.VMEM((4, ROWS, 128), BF16)] * 3,
            dma((10,)), dma((4,)),
            dma((3, 2, 4)), dma((3, 2, 4)),
            dma((4,)), dma((4,)), dma((3,)), dma((3,)),
            dma((4,)), dma((4,)),
            dma((2, 4)), dma((2, 4)), dma((2, 4, 3)), dma((2, 4, 3)),
        ],
        compiler_params=pltpu.CompilerParams(
            collective_id=0, has_side_effects=True, vmem_limit_bytes=48 << 20
        ),
        name="spread",
    )(q, k, v, og, w, mask)


def backward_kernel(
    q, g, k, v, fill, log_total, mean_t,
    dq_out, dk_out, dv_out,
    delta, dq_t, dq_part,
    held, core_got, z_part, z_got, part,
    local_sem, core_send, core_recv, z_send, z_recv, x_send, x_recv, q_send, q_recv,
):
    x, z, c, zh, y = place()

    def at_x(d):
        return device(lax.rem(x + d, 4), z, c, zh, y)

    core, zpeer = device(x, z, 1 - c, zh, y), device(x, 1 - z, c, zh, y)
    outs = (dk_out, dv_out)

    barrier = pltpu.get_barrier_semaphore()
    for peer in (at_x(1), at_x(2), at_x(3), core, zpeer):
        pl.semaphore_signal(barrier, inc=1, device_id=peer, device_id_type=MESH)

    delta[...] = jnp.sum(mean_t[...] * g[...].T.astype(F32), axis=0, keepdims=True)
    dq_t[...] = jnp.zeros_like(dq_t)

    pl.semaphore_wait(barrier, 5)

    def unit_grads(unit, slot, mine):
        rows = pl.ds(pl.multiple_of(unit * ROWS, ROWS), ROWS)
        k_unit = k[rows, :]
        p = jnp.exp2(unit_scores(k_unit, q, fill, unit, log_total[...]))
        prob_grad = lax.dot_general(v[rows, :], g[...], NT, preferred_element_type=F32)
        ds = (p * (prob_grad - delta[...])).astype(BF16)
        held[slot, mine, 1] = jnp.dot(p.astype(BF16), g[...], preferred_element_type=F32).astype(BF16)
        held[slot, mine, 0] = (jnp.dot(ds, q[...], preferred_element_type=F32) * SCALE).astype(BF16)
        dq_t[...] += jnp.dot(k_unit.T, ds, preferred_element_type=F32)

    def core_copy(slot, t):
        return remote(
            held.at[slot, 0, t], core_got.at[slot, t], core_send.at[slot, t], core_recv.at[slot, t], core)

    def z_copy(i, t):
        return remote(z_part.at[i, t], z_got.at[i, t], z_send.at[i, t], z_recv.at[i, t], zpeer)

    def x_copy(i, t):
        return remote(
            part.at[i, t], outs[t].at[:, head_lanes(x)], x_send.at[i, t], x_recv.at[i, t], at_x(i + 1))

    def summed(slot, t):
        core_copy(slot, t).wait_recv()
        return held[slot, 1, t].astype(F32) + core_got[slot, t].astype(F32)

    def finish(i):
        for t in range(2):
            mine = summed(4 + i, t)
            z_copy(i, t).wait_recv()
            part[i, t] = (mine + z_got[i, t].astype(F32)).astype(BF16)

    def step(slot, carry):
        xx = lax.rem(x + 1 + slot, 4)
        zz = jnp.where(slot < 4, 1 - z, z)

        def half(mine, carry):
            unit_grads(xx * 4 + zz * 2 + jnp.where(mine == 0, 1 - c, c), slot, mine)

            @pl.when(mine == 0)
            def _():
                for t in range(2):
                    core_copy(slot, t).start()

            return carry

        lax.fori_loop(0, 2, half, 0, unroll=True)

        @pl.when(slot < 4)
        def _():
            for t in range(2):
                z_part[slot, t] = summed(slot, t).astype(BF16)
                z_copy(slot, t).start()

        @pl.when(slot >= 4)
        def _():
            finish(slot - 4)
            for t in range(2):
                x_copy(slot - 4, t).start()

        return carry

    lax.fori_loop(0, 7, step, 0)

    def q_rows(xx):
        return pl.ds(pl.multiple_of(xx * ROWS, ROWS), ROWS)

    q_copies = [
        remote(
            dq_part.at[q_rows(lax.rem(x + d, 4))], dq_out.at[:, head_lanes(x)],
            q_send.at[d], q_recv.at[d], at_x(d))
        for d in (1, 2, 3)
    ]
    q_local = pltpu.make_async_copy(dq_part.at[q_rows(x)], dq_out.at[:, head_lanes(x)], local_sem.at[2])

    last = x * 2 + z
    last_rows = pl.ds(pl.multiple_of(last * 512, 512), 512)
    k_last, v_last = k[last_rows, :], v[last_rows, :]
    k_last_t = k_last.T
    sums = [0.0, 0.0]
    for j in range(4):
        tile = q_rows(lax.rem(x + 1 + j, 4))
        q_tile, g_tile = q[tile, :], g[tile, :]
        s = lax.dot_general(k_last, q_tile, NT, preferred_element_type=F32)
        p = jnp.exp2(jnp.concatenate(
            [
                s[a * BLOCK:(a + 1) * BLOCK] * (SCALE * LOG2E)
                + (fill[pl.ds(last * 4 + a, 1), tile] - log_total[:, tile])
                for a in range(4)
            ],
            axis=0,
        ))
        prob_grad = lax.dot_general(v_last, g_tile, NT, preferred_element_type=F32)
        ds = (p * (prob_grad - delta[:, tile])).astype(BF16)
        dq_tile = (dq_t[:, tile] + jnp.dot(k_last_t, ds, preferred_element_type=F32)) * SCALE
        dq_part[tile, :] = dq_tile.T.astype(BF16)
        if j < 3:
            q_copies[j].start()
        else:
            q_local.start()
        sums[0] += jnp.dot(ds, q_tile, preferred_element_type=F32)
        sums[1] += jnp.dot(p.astype(BF16), g_tile, preferred_element_type=F32)
    for t, total in enumerate((sums[0] * SCALE, sums[1])):
        held[7, 1 - c, t] = total[:ROWS].astype(BF16)
        held[7, c, t] = total[ROWS:].astype(BF16)
        core_copy(7, t).start()
    finish(3)
    for t in range(2):
        pltpu.make_async_copy(part.at[3, t], outs[t].at[:, head_lanes(x)], local_sem.at[t]).start()

    for i in range(3):
        lanes = head_lanes(lax.rem(x + 3 - i, 4))
        for t in range(2):
            dst = outs[t].at[:, lanes]
            remote(dst, dst, x_send.at[i, t], x_recv.at[i, t], core).wait_recv()
        dst = dq_out.at[:, lanes]
        remote(dst, dst, q_send.at[i + 1], q_recv.at[i + 1], core).wait_recv()
    q_local.wait()
    for t in range(2):
        pltpu.make_async_copy(part.at[3, t], outs[t].at[:, head_lanes(x)], local_sem.at[t]).wait()
        for i in range(3):
            x_copy(i, t).wait_send()
        for i in range(4):
            z_copy(i, t).wait_send()
        for slot in range(8):
            core_copy(slot, t).wait_send()
    for copy in q_copies:
        copy.wait_send()


def backward(*operands):
    dma = pltpu.SemaphoreType.DMA
    hbm = pl.BlockSpec(memory_space=pltpu.HBM)
    vmem = pl.BlockSpec(memory_space=pltpu.VMEM)
    piece = (2, ROWS, 128)
    lanes = NX * ROWS
    return pl.pallas_call(
        backward_kernel,
        out_shape=(jax.ShapeDtypeStruct((ROWS, 512), BF16),) * 3,
        in_specs=[vmem] * 7,
        out_specs=(hbm,) * 3,
        scratch_shapes=[
            pltpu.VMEM((1, lanes), F32),
            pltpu.VMEM((128, lanes), F32),
            pltpu.VMEM((lanes, 128), BF16),
            pltpu.VMEM((8, 2, *piece), BF16),
            pltpu.VMEM((8, *piece), BF16),
            *[pltpu.VMEM((4, *piece), BF16)] * 3,
            dma((3,)),
            dma((8, 2)), dma((8, 2)),
            dma((4, 2)), dma((4, 2)),
            dma((3, 2)), dma((3, 2)),
            dma((4,)), dma((4,)),
        ],
        compiler_params=pltpu.CompilerParams(
            collective_id=1, has_side_effects=True, vmem_limit_bytes=48 << 20
        ),
        name="backward",
    )(*operands)


def store_kernel(*refs):
    ins, outs, sem = refs[:3], refs[3:6], refs[6]
    copies = [pltpu.make_async_copy(a, b, sem.at[i]) for i, (a, b) in enumerate(zip(ins, outs))]
    for copy in copies:
        copy.start()
    for copy in copies:
        copy.wait()


def store(dq, dk, dv):
    anywhere = pl.BlockSpec(memory_space=pl.ANY)
    return pl.pallas_call(
        store_kernel,
        out_shape=(jax.ShapeDtypeStruct((ROWS, 512), BF16),) * 3,
        in_specs=[anywhere] * 3,
        out_specs=(anywhere,) * 3,
        scratch_shapes=[pltpu.SemaphoreType.DMA((3,))],
        compiler_params=pltpu.CompilerParams(vmem_limit_bytes=16 << 20),
        name="store",
    )(dq, dk, dv)


def per_device(query_proj, key_proj, value_proj, out_grad, out_weight, block_mask):
    query_proj, key_proj, value_proj, out_grad, block_mask = [
        pltpu.with_memory_space_constraint(a, pltpu.HBM)
        for a in (query_proj, key_proj, value_proj, out_grad, block_mask)
    ]
    q, k, v, g, fill, log_total, mean_t = spread(
        query_proj, key_proj, value_proj, out_grad, out_weight, block_mask
    )
    return store(*backward(q, g, k, v, fill, log_total, mean_t))


def solution(mesh):
    placed = (P("ctx", "tp"), P("ctx", "tp"), P("ctx", "tp"), P("ctx", "tp"), P(None, "tp"), P())
    return jax.shard_map(
        per_device,
        mesh=mesh,
        in_specs=placed,
        out_specs=(P("ctx", "tp"), P("ctx", "tp"), P("ctx", "tp")),
        check_vma=False,
    )
```

```python
import functools

import jax
import jax.numpy as jnp
from jax import lax
from jax.experimental import pallas as pl
from jax.experimental.pallas import tpu as pltpu
from jax.sharding import PartitionSpec as P

MESH = pl.DeviceIdType.MESH
HEAD_DIM = 128
BLOCK = 128
ROWS = 256
NX = 4
NB = 32
NEG_FILL = -1e30
SCALE = HEAD_DIM ** (-0.5)
LOG2E = 1.4426950408889634
BF16 = jnp.bfloat16
F32 = jnp.float32
NT = (((1,), (1,)), ((), ()))


def place():
    ctx, tp = lax.axis_index("ctx"), lax.axis_index("tp")
    return (
        lax.div(ctx, 4),
        lax.rem(lax.div(ctx, 2), 2),
        lax.rem(ctx, 2),
        lax.div(tp, 4),
        lax.rem(tp, 4),
    )


def device(x, z, c, zh, y):
    return {"ctx": x * 4 + z * 2 + c, "tp": zh * 4 + y}


def block_rows(x, z, c):
    return pl.ds(pl.multiple_of((x * 4 + z * 2 + c) * ROWS, ROWS), ROWS)


def head_lanes(h):
    return pl.ds(pl.multiple_of(h * HEAD_DIM, HEAD_DIM), HEAD_DIM)


def remote(src, dst, send, recv, to):
    return pltpu.make_async_remote_copy(
        src_ref=src, dst_ref=dst, send_sem=send, recv_sem=recv, device_id=to, device_id_type=MESH
    )


def fill_table(mask, fill, zc):
    block = lax.broadcasted_iota(jnp.int32, (NB, NX * ROWS), 0)
    lane = lax.broadcasted_iota(jnp.int32, (NB, NX * ROWS), 1)
    query_block = ((lane >> 8) * 4 + zc) * 2 + ((lane >> 7) & 1)
    own = jnp.where(block == query_block, 1.0, 0.0)
    may = jnp.where(mask[...] == 1, 1.0, 0.0)
    held = lax.dot_general(may, own, (((0,), (0,)), ((), ())), preferred_element_type=F32)
    fill[...] = jnp.where(held > 0.5, 0.0, NEG_FILL)


def unit_scores(k_unit, q, fill, unit, shift):
    s = lax.dot_general(k_unit, q[...], NT, preferred_element_type=F32)
    count = k_unit.shape[0] // BLOCK
    parts = [
        s[a * BLOCK:(a + 1) * BLOCK] * (SCALE * LOG2E) + (fill[pl.ds(unit * count + a, 1), :] - shift)
        for a in range(count)
    ]
    return jnp.concatenate(parts, axis=0)


def start_totals(totals, out_t):
    row = lax.broadcasted_iota(jnp.int32, totals.shape, 0)
    totals[...] = jnp.where(row == 0, NEG_FILL, 0.0)
    out_t[...] = jnp.zeros_like(out_t)


def add_totals(k, v, q, fill, totals, out_t, unit):
    rows = pl.ds(pl.multiple_of(unit * 512, 512), 512)
    s = unit_scores(k[rows, :], q, fill, unit, 0.0)
    old = totals[0:1, :]
    new = jnp.maximum(old, jnp.max(s, axis=0, keepdims=True))
    e = jnp.exp2(s - new)
    keep = jnp.exp2(old - new)
    totals[0:1, :] = new
    totals[1:2, :] = totals[1:2, :] * keep + jnp.sum(e, axis=0, keepdims=True)
    v_t = jnp.concatenate([v[rows, :].T, jnp.ones((16, 512), BF16)], axis=0)
    out_t[...] = out_t[...] * keep + jnp.dot(v_t, e.astype(BF16), preferred_element_type=F32)


def end_totals(totals, out_t, log_total, mean_t):
    log_total[...] = totals[0:1, :] + jnp.log(totals[1:2, :]) * LOG2E
    mean_t[...] = out_t[0:128, :] * (1.0 / out_t[128:129, :])


def spread_kernel(
    q_in, k_in, v_in, og_in, w_in, mask_in,
    q_out, k_out, v_out, g_out, fill, log_total, mean_t,
    mask, totals, out_t, og, w, own, relay, relay_got, comb, comb_got, direct, direct_got, z_part, z_got, g_part,
    load_sem, local_sem, y_send, y_recv, z_send, z_recv, g_send, g_recv,
    q_send, q_recv, kv_xsend, kv_xrecv, kv_fsend, kv_frecv,
):
    x, z, c, zh, y = place()
    yp, ym, yo = lax.rem(y + 1, 4), lax.rem(y + 3, 4), lax.rem(y + 2, 4)

    def at_x(d):
        return device(lax.rem(x + d, 4), z, c, zh, y)

    core, zpeer = device(x, z, 1 - c, zh, y), device(x, 1 - z, c, zh, y)
    up, down = device(x, z, c, zh, yp), device(x, z, c, zh, ym)
    zfar = device(x, z, c, 1 - zh, y)

    order = [(yo, 0), (yo, 1), (yp, 0), (ym, 1), (yp, 1), (ym, 0), (y, 0), (y, 1)]
    loads = [pltpu.make_async_copy(og_in, og, load_sem.at[8])]
    mask_load = pltpu.make_async_copy(mask_in, mask, load_sem.at[9])
    for i, (yy, zz) in enumerate(order):
        rows = pl.ds(pl.multiple_of((zz * 4 + yy) * 512, 512), 512)
        loads.append(pltpu.make_async_copy(w_in.at[rows], w.at[i], load_sem.at[i]))
    for load in loads:
        load.start()
    mask_load.start()

    barrier = pltpu.get_barrier_semaphore()
    for peer in (at_x(1), at_x(2), at_x(3), core, zpeer, up, down, zfar):
        pl.semaphore_signal(barrier, inc=1, device_id=peer, device_id_type=MESH)
    pl.semaphore_wait(barrier, 8)

    sent = []

    def go(copy):
        copy.start()
        sent.append(copy)

    def project(i):
        loads[1 + i].wait()
        return lax.dot_general(og[...], w[i], NT, preferred_element_type=F32)

    heads = [lax.rem(x + 1 + i, 4) for i in range(4)]

    def y_copy(kind, zz, i, src, dst, to):
        return remote(
            src.at[zz, heads[i]], dst.at[zz, heads[i]],
            y_send.at[kind, zz, i], y_recv.at[kind, zz, i], to,
        )

    turns = [[y_copy(0, zz, i, relay, relay_got, (up, down)[zz]) for zz in range(2)] for i in range(4)]
    for i in range(4):
        turns.append([y_copy(1, zz, i, comb, comb_got, (up, down)[zz]) for zz in range(2)])
        turns.append([y_copy(2, zz, i, direct, direct_got, (down, up)[zz]) for zz in range(2)])

    def turn(n):
        for copy in turns[n]:
            go(copy)

    loads[0].wait()
    for zz in range(2):
        part = project(zz)
        for h in range(4):
            relay[zz, h] = part[:, h * 128:(h + 1) * 128].astype(BF16)
    for n in range(4):
        turn(n)

    tensors = [(k_in, k_out), (v_in, v_out)]

    def kv_from_x(t, d):
        src, dst = tensors[t]
        return remote(
            src.at[:, head_lanes(lax.rem(x + d, 4))], dst.at[block_rows(x, z, c)],
            kv_xsend.at[t, d], kv_xrecv.at[t, d], at_x(d),
        )

    def kv_wait_x(t, d):
        dst = tensors[t][1].at[block_rows(lax.rem(x + 4 - d, 4), z, c)]
        remote(dst, dst, kv_xsend.at[t, d], kv_xrecv.at[t, d], core).wait_recv()

    def kv_forward(t, d, route):
        xs = lax.rem(x + 4 - d, 4)
        rows = block_rows(xs, z if route < 2 else 1 - z, c)
        dst = tensors[t][1].at[rows]
        src = tensors[t][0].at[:, head_lanes(x)] if (d == 0 and route < 2) else dst
        return remote(
            src, dst, kv_fsend.at[t, d, route], kv_frecv.at[t, d, route], zpeer if route == 1 else core
        )

    def kv_wait(t, d, route):
        xs = lax.rem(x + 4 - d, 4)
        rows = block_rows(xs, z if route == 0 else 1 - z, c if route == 1 else 1 - c)
        dst = tensors[t][1].at[rows]
        remote(dst, dst, kv_fsend.at[t, d, route], kv_frecv.at[t, d, route], core).wait_recv()

    for t in range(2):
        go(kv_forward(t, 0, 1))
    for d in (1, 3, 2):
        for t in range(2):
            go(kv_from_x(t, d))
    for t in range(2):
        go(kv_forward(t, 0, 0))
    local = []
    for t in range(2):
        local.append(pltpu.make_async_copy(
            tensors[t][0].at[:, head_lanes(x)], tensors[t][1].at[block_rows(x, z, c)], local_sem.at[t]))
    q_rows = pl.ds(pl.multiple_of(x * ROWS, ROWS), ROWS)
    local.append(pltpu.make_async_copy(q_in.at[:, head_lanes(x)], q_out.at[q_rows], local_sem.at[2]))
    for copy in local:
        copy.start()
    q_copies = [
        remote(q_in.at[:, head_lanes(lax.rem(x + d, 4))], q_out.at[q_rows], q_send.at[d], q_recv.at[d], at_x(d))
        for d in (1, 2, 3)
    ]

    for i in range(2, 8):
        zz = order[i][1]
        part = project(i)
        for h in range(4):
            piece = part[:, h * 128:(h + 1) * 128]
            if i in (4, 5):
                direct[zz, h] = piece.astype(BF16)
            else:
                own[0 if i < 4 else 1, zz, h] = piece

    def combine(i):
        h = heads[i]
        for zz in range(2):
            turns[i][zz].wait_recv()
            comb[zz, h] = (relay_got[zz, h].astype(F32) + own[0, zz, h]).astype(BF16)

    z_copies = [
        remote(z_part.at[heads[i]], z_got.at[heads[i]], z_send.at[i], z_recv.at[i], zfar) for i in range(4)
    ]

    def finish_y(i):
        h = heads[i]
        for zz in range(2):
            y_copy(1, zz, i, comb, comb_got, up).wait_recv()
            y_copy(2, zz, i, direct, direct_got, up).wait_recv()
        far = own[1, 1 - zh, h] + comb_got[1 - zh, h].astype(F32) + direct_got[1 - zh, h].astype(F32)
        z_part[h] = far.astype(BF16)
        go(z_copies[i])
        own[1, zh, h] = own[1, zh, h] + comb_got[zh, h].astype(F32) + direct_got[zh, h].astype(F32)

    def finish_z(i):
        h = heads[i]
        z_copies[i].wait_recv()
        g_part[h] = (own[1, zh, h] + z_got[h].astype(F32)).astype(BF16)
        if i < 3:
            go(remote(g_part.at[h], g_out.at[q_rows], g_send.at[i], g_recv.at[i], at_x(i + 1)))
        else:
            copy = pltpu.make_async_copy(g_part.at[h], g_out.at[q_rows], local_sem.at[3])
            copy.start()
            local.append(copy)

    def pass_on(d):
        for t in range(2):
            kv_wait_x(t, d)
            go(kv_forward(t, d, 1))
            go(kv_forward(t, d, 0))

    def pass_z(d):
        for t in range(2):
            kv_wait(t, d, 1)
            go(kv_forward(t, d, 2))

    for copy in q_copies:
        go(copy)
    mask_load.wait()
    fill_table(mask, fill, z * 2 + c)
    start_totals(totals, out_t)
    for i in range(4):
        combine(i)
        turn(4 + 2 * i)
        turn(5 + 2 * i)
        if i < 3:
            pass_on((1, 3, 2)[i])

    def add_units(distances, zz):
        def one(i, carry):
            d = distances[0] + i * (distances[-1] - distances[0])
            add_totals(k_out, v_out, q_out, fill, totals, out_t, lax.rem(x + 8 - d, 4) * 2 + zz)
            return carry

        lax.fori_loop(0, len(distances), one, 0, unroll=True)

    def await_core(d, route):
        for t in range(2):
            kv_wait(t, d, route)

    for copy in q_copies:
        copy.wait_recv()
    for copy in local:
        copy.wait()
    local.clear()
    await_core(0, 0)
    await_core(1, 0)
    add_units((0, 1), z)
    finish_y(0)
    pass_z(0)
    await_core(3, 0)
    await_core(2, 0)
    add_units((3, 2), z)
    pass_z(1)
    finish_y(1)
    finish_z(0)
    await_core(0, 2)
    await_core(1, 2)
    add_units((0, 1), 1 - z)
    pass_z(3)
    pass_z(2)
    finish_y(2)
    finish_z(1)
    await_core(3, 2)
    add_units((3,), 1 - z)
    finish_y(3)
    finish_z(2)
    await_core(2, 2)
    add_units((2,), 1 - z)
    end_totals(totals, out_t, log_total, mean_t)
    finish_z(3)

    for i in range(3):
        rows = pl.ds(pl.multiple_of(lax.rem(x + 3 - i, 4) * ROWS, ROWS), ROWS)
        dst = g_out.at[rows]
        remote(dst, dst, g_send.at[i], g_recv.at[i], core).wait_recv()
    for copy in local:
        copy.wait()
    for copy in sent:
        copy.wait_send()


def spread(q, k, v, og, w, mask):
    dma = pltpu.SemaphoreType.DMA
    hbm = pl.BlockSpec(memory_space=pltpu.HBM)
    vmem = pl.BlockSpec(memory_space=pltpu.VMEM)
    return pl.pallas_call(
        spread_kernel,
        out_shape=(
            jax.ShapeDtypeStruct((NX * ROWS, 128), BF16),
            jax.ShapeDtypeStruct((16 * ROWS, 128), BF16),
            jax.ShapeDtypeStruct((16 * ROWS, 128), BF16),
            jax.ShapeDtypeStruct((NX * ROWS, 128), BF16),
            jax.ShapeDtypeStruct((NB, NX * ROWS), F32),
            jax.ShapeDtypeStruct((1, NX * ROWS), F32),
            jax.ShapeDtypeStruct((128, NX * ROWS), F32),
        ),
        in_specs=[hbm] * 6,
        out_specs=(vmem,) * 7,
        scratch_shapes=[
            pltpu.VMEM((NB, NB), jnp.int32),
            pltpu.VMEM((8, NX * ROWS), F32),
            pltpu.VMEM((144, NX * ROWS), F32),
            pltpu.VMEM((ROWS, 512), BF16),
            pltpu.VMEM((8, 512, 512), BF16),
            pltpu.VMEM((2, 2, 4, ROWS, 128), F32),
            *[pltpu.VMEM((2, 4, ROWS, 128), BF16)] * 6,
            *[pltpu.VMEM((4, ROWS, 128), BF16)] * 3,
            dma((10,)), dma((4,)),
            dma((3, 2, 4)), dma((3, 2, 4)),
            dma((4,)), dma((4,)), dma((3,)), dma((3,)),
            dma((4,)), dma((4,)),
            dma((2, 4)), dma((2, 4)), dma((2, 4, 3)), dma((2, 4, 3)),
        ],
        compiler_params=pltpu.CompilerParams(
            collective_id=0, has_side_effects=True, vmem_limit_bytes=48 << 20
        ),
        name="spread",
    )(q, k, v, og, w, mask)


def backward_kernel(
    q, g, k, v, fill, log_total, mean_t,
    dq_out, dk_out, dv_out,
    delta, dq_t, dq_part,
    held, core_got, z_part, z_got, part,
    local_sem, core_send, core_recv, z_send, z_recv, x_send, x_recv, q_send, q_recv,
):
    x, z, c, zh, y = place()

    def at_x(d):
        return device(lax.rem(x + d, 4), z, c, zh, y)

    core, zpeer = device(x, z, 1 - c, zh, y), device(x, 1 - z, c, zh, y)
    outs = (dk_out, dv_out)

    barrier = pltpu.get_barrier_semaphore()
    for peer in (at_x(1), at_x(2), at_x(3), core, zpeer):
        pl.semaphore_signal(barrier, inc=1, device_id=peer, device_id_type=MESH)

    delta[...] = jnp.sum(mean_t[...] * g[...].T.astype(F32), axis=0, keepdims=True)
    dq_t[...] = jnp.zeros_like(dq_t)

    pl.semaphore_wait(barrier, 5)

    def unit_grads(unit, slot, mine):
        rows = pl.ds(pl.multiple_of(unit * ROWS, ROWS), ROWS)
        k_unit = k[rows, :]
        p = jnp.exp2(unit_scores(k_unit, q, fill, unit, log_total[...]))
        prob_grad = lax.dot_general(v[rows, :], g[...], NT, preferred_element_type=F32)
        ds = (p * (prob_grad - delta[...])).astype(BF16)
        held[slot, mine, 1] = jnp.dot(p.astype(BF16), g[...], preferred_element_type=F32).astype(BF16)
        held[slot, mine, 0] = (jnp.dot(ds, q[...], preferred_element_type=F32) * SCALE).astype(BF16)
        dq_t[...] += jnp.dot(k_unit.T, ds, preferred_element_type=F32)

    def core_copy(slot, t):
        return remote(
            held.at[slot, 0, t], core_got.at[slot, t], core_send.at[slot, t], core_recv.at[slot, t], core)

    def z_copy(i, t):
        return remote(z_part.at[i, t], z_got.at[i, t], z_send.at[i, t], z_recv.at[i, t], zpeer)

    def x_copy(i, t):
        return remote(
            part.at[i, t], outs[t].at[:, head_lanes(x)], x_send.at[i, t], x_recv.at[i, t], at_x(i + 1))

    def summed(slot, t):
        core_copy(slot, t).wait_recv()
        return held[slot, 1, t].astype(F32) + core_got[slot, t].astype(F32)

    def finish(i):
        for t in range(2):
            mine = summed(4 + i, t)
            z_copy(i, t).wait_recv()
            part[i, t] = (mine + z_got[i, t].astype(F32)).astype(BF16)

    def step(slot, carry):
        xx = lax.rem(x + 1 + slot, 4)
        zz = jnp.where(slot < 4, 1 - z, z)

        def half(mine, carry):
            unit_grads(xx * 4 + zz * 2 + jnp.where(mine == 0, 1 - c, c), slot, mine)

            @pl.when(mine == 0)
            def _():
                for t in range(2):
                    core_copy(slot, t).start()

            return carry

        lax.fori_loop(0, 2, half, 0, unroll=True)

        @pl.when(slot < 4)
        def _():
            for t in range(2):
                z_part[slot, t] = summed(slot, t).astype(BF16)
                z_copy(slot, t).start()

        @pl.when(slot >= 4)
        def _():
            finish(slot - 4)
            for t in range(2):
                x_copy(slot - 4, t).start()

        return carry

    lax.fori_loop(0, 7, step, 0)

    def q_rows(xx):
        return pl.ds(pl.multiple_of(xx * ROWS, ROWS), ROWS)

    q_copies = [
        remote(
            dq_part.at[q_rows(lax.rem(x + d, 4))], dq_out.at[:, head_lanes(x)],
            q_send.at[d], q_recv.at[d], at_x(d))
        for d in (1, 2, 3)
    ]
    q_local = pltpu.make_async_copy(dq_part.at[q_rows(x)], dq_out.at[:, head_lanes(x)], local_sem.at[2])

    last = x * 2 + z
    last_rows = pl.ds(pl.multiple_of(last * 512, 512), 512)
    k_last, v_last = k[last_rows, :], v[last_rows, :]
    k_last_t = k_last.T
    sums = [0.0, 0.0]
    for j in range(4):
        tile = q_rows(lax.rem(x + 1 + j, 4))
        q_tile, g_tile = q[tile, :], g[tile, :]
        s = lax.dot_general(k_last, q_tile, NT, preferred_element_type=F32)
        p = jnp.exp2(jnp.concatenate(
            [
                s[a * BLOCK:(a + 1) * BLOCK] * (SCALE * LOG2E)
                + (fill[pl.ds(last * 4 + a, 1), tile] - log_total[:, tile])
                for a in range(4)
            ],
            axis=0,
        ))
        prob_grad = lax.dot_general(v_last, g_tile, NT, preferred_element_type=F32)
        ds = (p * (prob_grad - delta[:, tile])).astype(BF16)
        dq_tile = (dq_t[:, tile] + jnp.dot(k_last_t, ds, preferred_element_type=F32)) * SCALE
        dq_part[tile, :] = dq_tile.T.astype(BF16)
        if j < 3:
            q_copies[j].start()
        else:
            q_local.start()
        sums[0] += jnp.dot(ds, q_tile, preferred_element_type=F32)
        sums[1] += jnp.dot(p.astype(BF16), g_tile, preferred_element_type=F32)
    for t, total in enumerate((sums[0] * SCALE, sums[1])):
        held[7, 1 - c, t] = total[:ROWS].astype(BF16)
        held[7, c, t] = total[ROWS:].astype(BF16)
        core_copy(7, t).start()
    finish(3)
    for t in range(2):
        pltpu.make_async_copy(part.at[3, t], outs[t].at[:, head_lanes(x)], local_sem.at[t]).start()

    for i in range(3):
        lanes = head_lanes(lax.rem(x + 3 - i, 4))
        for t in range(2):
            dst = outs[t].at[:, lanes]
            remote(dst, dst, x_send.at[i, t], x_recv.at[i, t], core).wait_recv()
        dst = dq_out.at[:, lanes]
        remote(dst, dst, q_send.at[i + 1], q_recv.at[i + 1], core).wait_recv()
    q_local.wait()
    for t in range(2):
        pltpu.make_async_copy(part.at[3, t], outs[t].at[:, head_lanes(x)], local_sem.at[t]).wait()
        for i in range(3):
            x_copy(i, t).wait_send()
        for i in range(4):
            z_copy(i, t).wait_send()
        for slot in range(8):
            core_copy(slot, t).wait_send()
    for copy in q_copies:
        copy.wait_send()


def backward(*operands):
    dma = pltpu.SemaphoreType.DMA
    hbm = pl.BlockSpec(memory_space=pltpu.HBM)
    vmem = pl.BlockSpec(memory_space=pltpu.VMEM)
    piece = (2, ROWS, 128)
    lanes = NX * ROWS
    return pl.pallas_call(
        backward_kernel,
        out_shape=(jax.ShapeDtypeStruct((ROWS, 512), BF16),) * 3,
        in_specs=[vmem] * 7,
        out_specs=(hbm,) * 3,
        scratch_shapes=[
            pltpu.VMEM((1, lanes), F32),
            pltpu.VMEM((128, lanes), F32),
            pltpu.VMEM((lanes, 128), BF16),
            pltpu.VMEM((8, 2, *piece), BF16),
            pltpu.VMEM((8, *piece), BF16),
            *[pltpu.VMEM((4, *piece), BF16)] * 3,
            dma((3,)),
            dma((8, 2)), dma((8, 2)),
            dma((4, 2)), dma((4, 2)),
            dma((3, 2)), dma((3, 2)),
            dma((4,)), dma((4,)),
        ],
        compiler_params=pltpu.CompilerParams(
            collective_id=1, has_side_effects=True, vmem_limit_bytes=48 << 20
        ),
        name="backward",
    )(*operands)


def store_kernel(*refs):
    ins, outs, sem = refs[:3], refs[3:6], refs[6]
    copies = [pltpu.make_async_copy(a, b, sem.at[i]) for i, (a, b) in enumerate(zip(ins, outs))]
    for copy in copies:
        copy.start()
    for copy in copies:
        copy.wait()


def store(dq, dk, dv):
    anywhere = pl.BlockSpec(memory_space=pl.ANY)
    return pl.pallas_call(
        store_kernel,
        out_shape=(jax.ShapeDtypeStruct((ROWS, 512), BF16),) * 3,
        in_specs=[anywhere] * 3,
        out_specs=(anywhere,) * 3,
        scratch_shapes=[pltpu.SemaphoreType.DMA((3,))],
        compiler_params=pltpu.CompilerParams(vmem_limit_bytes=16 << 20),
        name="store",
    )(dq, dk, dv)


def per_device(query_proj, key_proj, value_proj, out_grad, out_weight, block_mask):
    query_proj, key_proj, value_proj, out_grad, block_mask = [
        pltpu.with_memory_space_constraint(a, pltpu.HBM)
        for a in (query_proj, key_proj, value_proj, out_grad, block_mask)
    ]
    q, k, v, g, fill, log_total, mean_t = spread(
        query_proj, key_proj, value_proj, out_grad, out_weight, block_mask
    )
    return store(*backward(q, g, k, v, fill, log_total, mean_t))


def solution(mesh):
    placed = (P("ctx", "tp"), P("ctx", "tp"), P("ctx", "tp"), P("ctx", "tp"), P(None, "tp"), P())
    return jax.shard_map(
        per_device,
        mesh=mesh,
        in_specs=placed,
        out_specs=(P("ctx", "tp"), P("ctx", "tp"), P("ctx", "tp")),
        check_vma=False,
    )
```
